128 devices in a mesh: angle: 4 (over x), slab: 32 (over y, z, core).
Axes of the slice: x: 4, y: 4, z: 4, core: 2. Of those that a mesh axis runs over, the one named last changes fastest.
Arguments:
- projections: float32 [4, 4, 32, 4, 8192], P('angle', None, 'slab'), may hold values from -6 to 6
- band_start: int32 [4, 32], P('angle'), may hold values from 0 to 96
- row_index: int32 [4, 512, 4096], P('angle', 'slab'), may hold values from 0 to 126
- row_frac: float32 [4, 512, 4096], P('angle', 'slab'), may hold values from 0 to 1
- col_index: int32 [4, 4096], P('angle'), may hold values from 0 to 8190
- col_frac: float32 [4, 4096], P('angle'), may hold values from 0 to 1
- distance_weight: float32 [4, 4096], P('angle'), may hold values from 0.5 to 2
Outputs:
- volume: float32 [512, 4096], P('slab', 'angle')
The draws below stay inside these ranges and needn't reach their ends.
All inputs are finite; a program needn't handle non-finite values.
Results may differ from the reference program's by a relative error of at most 0.0034.
Values may be sent and summed in bfloat16 or wider, within the bound.
A program may use at most 128 MiB of HBM per device.

```python
import math
import jax
import jax.numpy as jnp
from jax import lax

COLS = 8192
BAND = 4
BANDS_DEV = 4
PLANES = 16
VOX = 4096
PROJ_ALL = 4
PLANES_ALL = 512
DET_ROWS = 512
WIN = 128
N_SLAB = 32


def touch_ends(drawn, stream_key, low, largest):
    longest = drawn.shape.index(max(drawn.shape))
    spots = []
    for shift in (0, 1):
        where = [jax.random.randint(jax.random.fold_in(stream_key, axis), (), 0, length) for axis, length in enumerate(drawn.shape)]
        where[longest] = (where[longest] + shift) % drawn.shape[longest]
        spots.append(tuple(where))
    return drawn.at[spots[0]].set(low).at[spots[1]].set(largest)


def levels(rng, dims, split, smallest, largest):
    gain, own = 1.0, jax.random.fold_in(rng, 6)
    for position, parts in split:
        heights = jnp.exp(jax.random.uniform(jax.random.fold_in(own, position), (parts,), jnp.float32, smallest / len(split), largest / len(split)))
        gain = gain * jnp.repeat(heights, dims[position] // parts).reshape([-1 if axis == position else 1 for axis in range(len(dims))])
    return gain


def noise(own_key, dims, scale, bound, split=(), kind=jnp.bfloat16):
    gain = levels(own_key, dims, split, -0.22, 0.18) if split else 1.0
    result = jax.random.normal(own_key, dims, jnp.float32) * scale * gain
    return jnp.minimum(jnp.maximum(result, -bound), bound).astype(kind)


def setup_inputs(seed: int = 0) -> dict:
    keys = jax.random.split(jax.random.key(seed), 8)
    return {
        "projections": noise(keys[0], (PROJ_ALL, BANDS_DEV, N_SLAB, BAND, COLS), 1.0, 6.0, ((0, 4), (2, 32)), jnp.float32),
        "band_start": touch_ends(jax.random.randint(keys[1], (PROJ_ALL, N_SLAB), 0, BANDS_DEV * N_SLAB - N_SLAB + 1), jax.random.fold_in(keys[1], 1), 0, BANDS_DEV * N_SLAB - N_SLAB).astype(jnp.int32),
        "row_index": touch_ends(jax.random.randint(keys[2], (PROJ_ALL, PLANES_ALL, VOX), 0, N_SLAB * BAND - 1), jax.random.fold_in(keys[2], 1), 0, (N_SLAB * BAND - 1) - 1).astype(jnp.int32),
        "row_frac": jnp.clip(1.0 * jax.random.uniform(keys[3], (PROJ_ALL, PLANES_ALL, VOX), jnp.float32) ** levels(keys[3], (PROJ_ALL, PLANES_ALL, VOX), ((0, 4), (1, 32)), -0.2, 0.2), 0.0, 1.0),
        "col_index": touch_ends(jax.random.randint(keys[4], (PROJ_ALL, VOX), 0, COLS - 1), jax.random.fold_in(keys[4], 1), 0, (COLS - 1) - 1).astype(jnp.int32),
        "col_frac": jnp.clip(1.0 * jax.random.uniform(keys[5], (PROJ_ALL, VOX), jnp.float32) ** levels(keys[5], (PROJ_ALL, VOX), ((0, 4),), -0.2, 0.2), 0.0, 1.0),
        "distance_weight": jnp.clip(jnp.exp(math.log(2.0) - 1.3862944 * jax.random.uniform(keys[6], (PROJ_ALL, VOX), jnp.float32) ** levels(keys[6], (PROJ_ALL, VOX), ((0, 4),), -0.2, 0.2)), 0.5, 2.0),
    }


def ramp_kernel(cols):
    total = 2 * cols
    steps = jnp.arange(total, dtype=jnp.int32)
    dist = jnp.minimum(steps, total - steps)
    safe = jnp.maximum(dist, 1).astype(jnp.float32)
    odd_value = -1.0 / (math.pi ** 2 * safe * safe)
    kernel = jnp.where(dist == 0, jnp.float32(0.25), jnp.where(dist % 2 == 1, odd_value, jnp.float32(0.0)))
    return kernel.astype(jnp.float32)

def cos_weight(det_rows, cols, det_total):
    scale = 2.0 * cols
    across = jnp.arange(cols, dtype=jnp.float32) - (cols - 1) / 2.0
    down = det_rows.astype(jnp.float32) - (det_total - 1) / 2.0
    return scale / jnp.sqrt(scale * scale + across * across + down[..., None] * down[..., None])

def reference(projections, band_start, row_index, row_frac, col_index, col_frac, distance_weight):
    total = 2 * COLS
    rows = projections.reshape(PROJ_ALL, DET_ROWS, COLS)
    weighted = rows * cos_weight(jnp.arange(DET_ROWS, dtype=jnp.int32), COLS, DET_ROWS)[None]
    response = jnp.fft.rfft(ramp_kernel(COLS)).real

    def filter_one(image):
        padded = jnp.pad(image, ((0, 0), (0, COLS)))
        spectrum = jnp.fft.rfft(padded, axis=-1) * response[None, :]
        return jnp.fft.irfft(spectrum, n=total, axis=-1)[:, :COLS].astype(jnp.bfloat16)
    filtered = lax.map(filter_one, weighted)
    plane_slab = (jnp.arange(PLANES_ALL, dtype=jnp.int32) // PLANES)[:, None]

    def add_one(volume, items):
        image, starts, rows_at, rows_frac, cols_at, cols_frac, weights = items
        row_ids = starts[:, None] * BAND + jnp.arange(WIN, dtype=jnp.int32)[None, :]
        window = image[row_ids]
        cols_wide = cols_at[None, :]
        low_left = window[plane_slab, rows_at, cols_wide].astype(jnp.float32)
        low_right = window[plane_slab, rows_at, cols_wide + 1].astype(jnp.float32)
        high_left = window[plane_slab, rows_at + 1, cols_wide].astype(jnp.float32)
        high_right = window[plane_slab, rows_at + 1, cols_wide + 1].astype(jnp.float32)
        across = cols_frac[None, :]
        lower = (1.0 - across) * low_left + across * low_right
        upper = (1.0 - across) * high_left + across * high_right
        mixed = (1.0 - rows_frac) * lower + rows_frac * upper
        return (volume + weights[None, :] * mixed, None)
    start_volume = jnp.zeros((PLANES_ALL, VOX), jnp.float32)
    volume, unused = lax.scan(add_one, start_volume, (filtered, band_start, row_index, row_frac, col_index, col_frac, distance_weight))
    return volume
```

```python
import math

import jax
import jax.numpy as jnp
from jax import lax
from jax.experimental import pallas as pl
from jax.experimental.pallas import tpu as pltpu
from jax.sharding import PartitionSpec as P

F32 = jnp.float32
BF16 = jnp.bfloat16
I32 = jnp.int32
MESH = pl.DeviceIdType.MESH

ANGLES = 4
SLABS = 32
BANDS = 4
BAND = 4
ROWS = 16
COLS = 8192
DET = 512
PLANES = 16
VOX = 4096
OUT_VOX = 1024
SUB = 256
BLOCKS = 16
HALF = COLS // 2
TOEP_LO = -(BLOCKS - 1) * SUB - 128
TOEP_WIDTH = (2 * BLOCKS - 1) * SUB + 128
TILE = 512


def split_hi_lo(value):
    high = value.astype(BF16)
    low = (value - high.astype(F32)).astype(BF16)
    return high, low


def ramp_odd(offset):
    step = (2 * offset - 1).astype(F32)
    return (-1.0 / math.pi**2) / (step * step)


def make_toeplitz(toep_hi, toep_lo):
    lane = lax.broadcasted_iota(I32, (128, 128), 1)
    sub = lax.broadcasted_iota(I32, (128, 128), 0)
    base = lane - sub + TOEP_LO

    def one(j, carry):
        high, low = split_hi_lo(ramp_odd(base + j * 128))
        where = pl.ds(pl.multiple_of(j * 128, 128), 128)
        toep_hi[:, where] = high
        toep_lo[:, where] = low
        return carry

    lax.fori_loop(0, TOEP_WIDTH // 128, one, 0)


def load_weighted(slab, x_ref, xs_hi, xs_lo):
    scale = 2.0 * COLS
    row = lax.broadcasted_iota(I32, (ROWS, SUB), 0)
    lane = lax.broadcasted_iota(I32, (ROWS, SUB), 1)
    det = ((row // BAND) * SLABS + slab) * BAND + row % BAND
    down = det.astype(F32) - (DET - 1) / 2.0
    rest = scale * scale + down * down
    for kb in range(COLS // SUB):
        across = (lane + kb * SUB).astype(F32) - (COLS - 1) / 2.0
        raw = jnp.concatenate(
            [x_ref[b, :, kb * SUB : (kb + 1) * SUB] for b in range(BANDS)], axis=0
        )
        high, low = split_hi_lo(raw * (scale / jnp.sqrt(rest + across * across)))
        xs_hi[kb * ROWS : (kb + 1) * ROWS, :] = high
        xs_lo[kb * ROWS : (kb + 1) * ROWS, :] = low
    xs_hi[2 * SUB :, :] = jnp.zeros((ROWS, SUB), BF16)
    xs_lo[2 * SUB :, :] = jnp.zeros((ROWS, SUB), BF16)


def one_hot(mask):
    return jnp.where(mask, 1.0, 0.0).astype(BF16)


def split_parity(xs_hi, xs_lo, z_hi, z_lo, y_ref):
    k = lax.broadcasted_iota(I32, (SUB, SUB), 0)
    n = lax.broadcasted_iota(I32, (SUB, SUB), 1)
    even_odd = one_hot(k == jnp.where(n < 128, 2 * n, 2 * n - 255))
    k2 = lax.broadcasted_iota(I32, (2 * SUB, 128), 0)
    n2 = lax.broadcasted_iota(I32, (2 * SUB, 128), 1)
    later = one_hot(k2 == 2 * n2 + 2)
    first = None
    quarter = None
    for xs, z in ((xs_hi, z_hi), (xs_lo, z_lo)):
        here = xs[: 2 * SUB, :]
        both = jnp.concatenate([here, xs[ROWS : 2 * SUB + ROWS, :]], axis=1)
        eo = jnp.dot(here, even_odd, preferred_element_type=F32)
        es = jnp.dot(both, later, preferred_element_type=F32).astype(BF16)
        eo_b = eo[:, 128:].astype(BF16)
        for kb in range(2 * BLOCKS):
            mb, half = kb // 2, kb % 2
            lanes = slice(half * 128, half * 128 + 128)
            src = slice(kb * ROWS, (kb + 1) * ROWS)
            z[mb * 32 : mb * 32 + 16, lanes] = eo_b[src]
            z[mb * 32 + 16 : mb * 32 + 32, lanes] = es[src]
        quarter = eo if quarter is None else quarter + eo
        first = eo[:ROWS, 0:1] if first is None else first + eo[:ROWS, 0:1]
    quarter = quarter * 0.25
    lane = lax.broadcasted_iota(I32, (ROWS, 128), 1)
    for kb in range(2 * BLOCKS):
        mb, half = kb // 2, kb % 2
        lanes = slice(half * 128, half * 128 + 128)
        src = slice(kb * ROWS, (kb + 1) * ROWS)
        y_ref[mb * 32 : mb * 32 + 16, lanes] = quarter[src, :128]
        edge = first * ramp_odd(lane + (kb * 128 + 1))
        y_ref[mb * 32 + 16 : mb * 32 + 32, lanes] = quarter[src, 128:] + edge


def convolve(toep_hi, toep_lo, z_hi, z_lo, y_ref):
    for d in range(-(BLOCKS - 1), BLOCKS):
        at = d * SUB - TOEP_LO
        count = (BLOCKS - abs(d)) * 32
        src = slice(max(0, -d) * 32, max(0, -d) * 32 + count)
        dst = slice(max(0, d) * 32, max(0, d) * 32 + count)
        t_hi = jnp.concatenate(
            [toep_hi[:, at : at + SUB], toep_hi[:, at - 128 : at + 128]], axis=0
        )
        t_lo = jnp.concatenate(
            [toep_lo[:, at : at + SUB], toep_lo[:, at - 128 : at + 128]], axis=0
        )
        part = (
            jnp.dot(z_hi[src, :], t_hi, preferred_element_type=F32)
            + jnp.dot(z_lo[src, :], t_hi, preferred_element_type=F32)
            + jnp.dot(z_hi[src, :], t_lo, preferred_element_type=F32)
        )
        y_ref[dst, :] += part


def round_filtered(y_ref, f_even, f_odd):
    for mb in range(BLOCKS):
        f_even[mb * 16 : mb * 16 + 16, :] = y_ref[mb * 32 : mb * 32 + 16, :].astype(BF16)
        f_odd[mb * 16 : mb * 16 + 16, :] = y_ref[mb * 32 + 16 : mb * 32 + 32, :].astype(BF16)


def pick_columns(f_ref, index):
    low = jnp.bitwise_and(index, SUB - 1)
    high = lax.shift_right_logical(index, 8)
    row = lax.broadcasted_iota(I32, (SUB, TILE), 0)
    hot = one_hot(row == low)
    wide = jnp.dot(f_ref[...], hot, preferred_element_type=F32)
    high16 = jnp.broadcast_to(high, (ROWS, TILE))
    got = wide[:ROWS]
    for mb in range(1, BLOCKS):
        got = jnp.where(high16 == mb, wide[mb * ROWS : (mb + 1) * ROWS], got)
    return got


def interpolate_columns(at, f_even, f_odd, c_ref, b_ref, w_ref):
    where = pl.ds(at, TILE)
    column = c_ref[:, where]
    frac = b_ref[:, where]
    weight = w_ref[:, where]
    odd = jnp.bitwise_and(column, 1) == 1
    even_weight = jnp.where(odd, frac, 1.0 - frac) * weight
    odd_weight = jnp.where(odd, 1.0 - frac, frac) * weight
    even_part = pick_columns(f_even, lax.shift_right_logical(column + 1, 1))
    odd_part = pick_columns(f_odd, lax.shift_right_logical(column, 1))
    return even_part * even_weight + odd_part * odd_weight


def kernel(
    x_hbm, start_hbm, rows_hbm, frac_hbm, col_hbm, colf_hbm, dist_hbm, out_ref,
    x_v, start_v, rows_v, frac_v, col_v, colf_v, dist_v,
    toep_hi, toep_lo, xs_hi, xs_lo, z_hi, z_lo, y_ref, f_even, f_odd,
    s_send, s_recv, h_send, h_recv, o_send, o_recv, st_ref,
    in_sem, s_ssem, s_rsem, h_ssem, h_rsem, o_ssem, o_rsem,
):
    angle = lax.axis_index("angle")
    slab = lax.axis_index("slab")
    owner = slab // 8
    seat = slab % 8
    at_home = owner == angle

    barrier = pltpu.get_barrier_semaphore()

    def greet_slab(o, carry):
        pl.semaphore_signal(
            barrier, inc=1, device_id=(angle, lax.rem(slab + o, SLABS)), device_id_type=MESH
        )
        return carry

    lax.fori_loop(1, SLABS, greet_slab, 0)

    def greet_sender(o, carry):
        other_angle = o // 8
        other_slab = angle * 8 + o % 8
        mine = jnp.logical_and(other_angle == angle, other_slab == slab)

        @pl.when(jnp.logical_not(mine))
        def _():
            pl.semaphore_signal(
                barrier, inc=1, device_id=(other_angle, other_slab), device_id_type=MESH
            )

        return carry

    lax.fori_loop(0, 32, greet_sender, 0)

    loads = [
        pltpu.make_async_copy(src, dst, in_sem.at[i])
        for i, (src, dst) in enumerate(
            (
                (start_hbm, start_v),
                (rows_hbm, rows_v),
                (frac_hbm, frac_v),
                (x_hbm, x_v),
                (col_hbm, col_v),
                (colf_hbm, colf_v),
                (dist_hbm, dist_v),
            )
        )
    ]
    for load in loads:
        load.start()

    for load in loads[:3]:
        load.wait()
    lane32 = lax.broadcasted_iota(I32, (1, SLABS), 1)
    first_row = BAND * jnp.sum(jnp.where(lane32 == slab, start_v[...], 0), axis=1, keepdims=True)
    for t in range(SLABS):
        lanes = slice(t * 128, t * 128 + 128)
        s_send[t] = (rows_v[:, lanes] + first_row).astype(F32) + frac_v[:, lanes]

    @pl.when(at_home)
    def _():
        pl.semaphore_wait(barrier, 62)

    @pl.when(jnp.logical_not(at_home))
    def _():
        pl.semaphore_wait(barrier, 63)

    def send_rows(o, carry):
        peer = lax.rem(slab + o, SLABS)
        pltpu.make_async_remote_copy(
            src_ref=s_send.at[peer], dst_ref=s_recv.at[slab],
            send_sem=s_ssem, recv_sem=s_rsem,
            device_id=(angle, peer), device_id_type=MESH,
        ).start()
        return carry

    lax.fori_loop(1, SLABS, send_rows, 0)
    s_recv[slab] = s_send[slab]

    make_toeplitz(toep_hi, toep_lo)
    for load in loads[3:]:
        load.wait()
    load_weighted(slab, x_v, xs_hi, xs_lo)
    split_parity(xs_hi, xs_lo, z_hi, z_lo, y_ref)
    convolve(toep_hi, toep_lo, z_hi, z_lo, y_ref)
    round_filtered(y_ref, f_even, f_odd)

    def columns(i, carry):
        at = pl.multiple_of(i * TILE, TILE)
        value = interpolate_columns(at, f_even, f_odd, col_v, colf_v, dist_v).astype(BF16)
        for j in range(TILE // 128):
            h_send[i * (TILE // 128) + j] = value[:, j * 128 : (j + 1) * 128]
        return carry

    lax.fori_loop(0, VOX // TILE, columns, 0)

    def send_columns(o, carry):
        peer = lax.rem(slab + o, SLABS)
        pltpu.make_async_remote_copy(
            src_ref=h_send.at[peer], dst_ref=h_recv.at[slab],
            send_sem=h_ssem, recv_sem=h_rsem,
            device_id=(angle, peer), device_id_type=MESH,
        ).start()
        return carry

    lax.fori_loop(1, SLABS, send_columns, 0)
    h_recv[slab] = h_send[slab]

    def wait_bytes(ref, count, sem):
        pltpu.make_async_copy(ref.at[pl.ds(0, count)], ref.at[pl.ds(0, count)], sem).wait()

    wait_bytes(s_recv, SLABS - 1, s_rsem)
    for g in range(4):
        st_ref[:, g * 128 : (g + 1) * 128] = (
            s_recv[g * 8 : (g + 1) * 8].reshape(128, 128).T
        )

    wait_bytes(h_recv, SLABS - 1, h_rsem)
    tables = [
        h_recv[g * 8 : (g + 1) * 8].reshape(128, 128).astype(F32).T for g in range(4)
    ]
    for g in range(4):
        pieces = []
        for v in range(16):
            position = st_ref[v * 8 : v * 8 + 8, g * 128 : (g + 1) * 128]
            row = position.astype(I32)
            frac = position - row.astype(F32)
            values = []
            for r in (row, jnp.minimum(row + 1, DET - 1)):
                lane = (
                    jnp.bitwise_and(lax.shift_right_logical(r, 2), 7) * 16
                    + lax.shift_right_logical(r, 7) * 4
                    + jnp.bitwise_and(r, 3)
                )
                which = jnp.bitwise_and(lax.shift_right_logical(r, 5), 3)
                got = None
                for k in range(4):
                    part = jnp.take_along_axis(
                        tables[k][v * 8 : v * 8 + 8], lane, axis=1, mode="promise_in_bounds"
                    )
                    got = part if got is None else jnp.where(which == k, part, got)
                values.append(got)
            pieces.append((1.0 - frac) * values[0] + frac * values[1])
        o_send[g * 8 : (g + 1) * 8] = jnp.concatenate(pieces, axis=0).T.reshape(8, 16, 128)

    slot = angle * 8 + seat

    def send_planes(o, carry):
        t = lax.rem(slab + o, SLABS)
        mine = jnp.logical_and(at_home, o == 0)

        @pl.when(jnp.logical_not(mine))
        def _():
            pltpu.make_async_remote_copy(
                src_ref=o_send.at[t], dst_ref=o_recv.at[slot],
                send_sem=o_ssem, recv_sem=o_rsem,
                device_id=(owner, t), device_id_type=MESH,
            ).start()

        return carry

    lax.fori_loop(0, SLABS, send_planes, 0)

    @pl.when(at_home)
    def _():
        o_recv[slot] = o_send[slab]
        wait_bytes(o_recv, 31, o_rsem)

    @pl.when(jnp.logical_not(at_home))
    def _():
        wait_bytes(o_recv, 32, o_rsem)

    for k in range(8):
        out_ref[:, k * 128 : (k + 1) * 128] = (
            o_recv[k] + o_recv[8 + k] + o_recv[16 + k] + o_recv[24 + k]
        )

    wait_bytes(s_send, SLABS - 1, s_ssem)
    wait_bytes(h_send, SLABS - 1, h_ssem)

    @pl.when(at_home)
    def _():
        wait_bytes(o_send, 31, o_ssem)

    @pl.when(jnp.logical_not(at_home))
    def _():
        wait_bytes(o_send, 32, o_ssem)


SCRATCH = [
    pltpu.VMEM((BANDS, BAND, COLS), F32),
    pltpu.VMEM((1, SLABS), I32),
    pltpu.VMEM((PLANES, VOX), I32),
    pltpu.VMEM((PLANES, VOX), F32),
    pltpu.VMEM((1, VOX), I32),
    pltpu.VMEM((1, VOX), F32),
    pltpu.VMEM((1, VOX), F32),
    pltpu.VMEM((128, TOEP_WIDTH), BF16),
    pltpu.VMEM((128, TOEP_WIDTH), BF16),
    pltpu.VMEM((2 * SUB + ROWS, SUB), BF16),
    pltpu.VMEM((2 * SUB + ROWS, SUB), BF16),
    pltpu.VMEM((2 * SUB, SUB), BF16),
    pltpu.VMEM((2 * SUB, SUB), BF16),
    pltpu.VMEM((2 * SUB, SUB), F32),
    pltpu.VMEM((SUB, SUB), BF16),
    pltpu.VMEM((SUB, SUB), BF16),
    pltpu.VMEM((SLABS, PLANES, 128), F32),
    pltpu.VMEM((SLABS, PLANES, 128), F32),
    pltpu.VMEM((SLABS, ROWS, 128), BF16),
    pltpu.VMEM((SLABS, ROWS, 128), BF16),
    pltpu.VMEM((SLABS, PLANES, 128), F32),
    pltpu.VMEM((SLABS, PLANES, 128), F32),
    pltpu.VMEM((128, SLABS * PLANES), F32),
    pltpu.SemaphoreType.DMA((7,)),
    pltpu.SemaphoreType.DMA,
    pltpu.SemaphoreType.DMA,
    pltpu.SemaphoreType.DMA,
    pltpu.SemaphoreType.DMA,
    pltpu.SemaphoreType.DMA,
    pltpu.SemaphoreType.DMA,
]


def body(projections, band_start, row_index, row_frac, col_index, col_frac, distance_weight):
    call = pl.pallas_call(
        kernel,
        out_shape=jax.ShapeDtypeStruct((PLANES, OUT_VOX), F32),
        in_specs=[pl.BlockSpec(memory_space=pl.ANY)] * 7,
        out_specs=pl.BlockSpec(memory_space=pltpu.VMEM),
        scratch_shapes=SCRATCH,
        compiler_params=pltpu.CompilerParams(
            collective_id=0, has_side_effects=True, vmem_limit_bytes=40 * 1024 * 1024
        ),
        cost_estimate=pl.CostEstimate(
            flops=6 * 10**9, bytes_accessed=2 * 10**6, transcendentals=0
        ),
    )
    return call(
        projections.reshape(BANDS, BAND, COLS),
        band_start,
        row_index.reshape(PLANES, VOX),
        row_frac.reshape(PLANES, VOX),
        col_index,
        col_frac,
        distance_weight,
    )


def solution(mesh):
    in_specs = (
        P("angle", None, "slab", None, None),
        P("angle", None),
        P("angle", "slab", None),
        P("angle", "slab", None),
        P("angle", None),
        P("angle", None),
        P("angle", None),
    )
    out_specs = P("slab", "angle")
    return jax.shard_map(body, mesh=mesh, in_specs=in_specs, out_specs=out_specs, check_vma=False)
```

```python
import math

import jax
import jax.numpy as jnp
from jax import lax
from jax.experimental import pallas as pl
from jax.experimental.pallas import tpu as pltpu
from jax.sharding import PartitionSpec as P

F32 = jnp.float32
BF16 = jnp.bfloat16
I32 = jnp.int32
MESH = pl.DeviceIdType.MESH

ANGLES = 4
OWNERS = 4
SLABS = 32
BANDS = 4
BAND = 4
ROWS = 16
COLS = 8192
DET = 512
PLANES = 16
VOX = 4096
OUT_VOX = 1024
SUB = 256
BLOCKS = 16
HALF = COLS // 2
TOEP_LO = -(BLOCKS - 1) * SUB - 128
TOEP_WIDTH = (2 * BLOCKS - 1) * SUB + 128
TILE = 512


def split_hi_lo(value):
    high = value.astype(BF16)
    low = (value - high.astype(F32)).astype(BF16)
    return high, low


def ramp_odd(offset):
    step = (2 * offset - 1).astype(F32)
    return (-1.0 / math.pi**2) / (step * step)


def make_toeplitz(toep_hi, toep_lo):
    lane = lax.broadcasted_iota(I32, (128, 128), 1)
    sub = lax.broadcasted_iota(I32, (128, 128), 0)
    base = lane - sub + TOEP_LO

    def one(j, carry):
        high, low = split_hi_lo(ramp_odd(base + j * 128))
        where = pl.ds(pl.multiple_of(j * 128, 128), 128)
        toep_hi[:, where] = high
        toep_lo[:, where] = low
        return carry

    lax.fori_loop(0, TOEP_WIDTH // 128, one, 0)


def load_weighted(slab, x_ref, xs_hi, xs_lo):
    scale = 2.0 * COLS
    row = lax.broadcasted_iota(I32, (ROWS, SUB), 0)
    lane = lax.broadcasted_iota(I32, (ROWS, SUB), 1)
    det = ((row // BAND) * SLABS + slab) * BAND + row % BAND
    down = det.astype(F32) - (DET - 1) / 2.0
    rest = scale * scale + down * down
    for kb in range(COLS // SUB):
        across = (lane + kb * SUB).astype(F32) - (COLS - 1) / 2.0
        raw = jnp.concatenate(
            [x_ref[b, :, kb * SUB : (kb + 1) * SUB] for b in range(BANDS)], axis=0
        )
        high, low = split_hi_lo(raw * (scale / jnp.sqrt(rest + across * across)))
        xs_hi[kb * ROWS : (kb + 1) * ROWS, :] = high
        xs_lo[kb * ROWS : (kb + 1) * ROWS, :] = low
    xs_hi[2 * SUB :, :] = jnp.zeros((ROWS, SUB), BF16)
    xs_lo[2 * SUB :, :] = jnp.zeros((ROWS, SUB), BF16)


def one_hot(mask):
    return jnp.where(mask, 1.0, 0.0).astype(BF16)


def split_parity(xs_hi, xs_lo, z_hi, z_lo, y_ref):
    k = lax.broadcasted_iota(I32, (SUB, SUB), 0)
    n = lax.broadcasted_iota(I32, (SUB, SUB), 1)
    even_odd = one_hot(k == jnp.where(n < 128, 2 * n, 2 * n - 255))
    k2 = lax.broadcasted_iota(I32, (2 * SUB, 128), 0)
    n2 = lax.broadcasted_iota(I32, (2 * SUB, 128), 1)
    later = one_hot(k2 == 2 * n2 + 2)
    first = None
    quarter = None
    for xs, z in ((xs_hi, z_hi), (xs_lo, z_lo)):
        here = xs[: 2 * SUB, :]
        both = jnp.concatenate([here, xs[ROWS : 2 * SUB + ROWS, :]], axis=1)
        eo = jnp.dot(here, even_odd, preferred_element_type=F32)
        es = jnp.dot(both, later, preferred_element_type=F32).astype(BF16)
        eo_b = eo[:, 128:].astype(BF16)
        for kb in range(2 * BLOCKS):
            mb, half = kb // 2, kb % 2
            lanes = slice(half * 128, half * 128 + 128)
            src = slice(kb * ROWS, (kb + 1) * ROWS)
            z[mb * 32 : mb * 32 + 16, lanes] = eo_b[src]
            z[mb * 32 + 16 : mb * 32 + 32, lanes] = es[src]
        quarter = eo if quarter is None else quarter + eo
        first = eo[:ROWS, 0:1] if first is None else first + eo[:ROWS, 0:1]
    quarter = quarter * 0.25
    lane = lax.broadcasted_iota(I32, (ROWS, 128), 1)
    for kb in range(2 * BLOCKS):
        mb, half = kb // 2, kb % 2
        lanes = slice(half * 128, half * 128 + 128)
        src = slice(kb * ROWS, (kb + 1) * ROWS)
        y_ref[mb * 32 : mb * 32 + 16, lanes] = quarter[src, :128]
        edge = first * ramp_odd(lane + (kb * 128 + 1))
        y_ref[mb * 32 + 16 : mb * 32 + 32, lanes] = quarter[src, 128:] + edge


def convolve(toep_hi, toep_lo, z_hi, z_lo, y_ref):
    for d in range(-(BLOCKS - 1), BLOCKS):
        at = d * SUB - TOEP_LO
        count = (BLOCKS - abs(d)) * 32
        src = slice(max(0, -d) * 32, max(0, -d) * 32 + count)
        dst = slice(max(0, d) * 32, max(0, d) * 32 + count)
        t_hi = jnp.concatenate(
            [toep_hi[:, at : at + SUB], toep_hi[:, at - 128 : at + 128]], axis=0
        )
        t_lo = jnp.concatenate(
            [toep_lo[:, at : at + SUB], toep_lo[:, at - 128 : at + 128]], axis=0
        )
        part = (
            jnp.dot(z_hi[src, :], t_hi, preferred_element_type=F32)
            + jnp.dot(z_lo[src, :], t_hi, preferred_element_type=F32)
            + jnp.dot(z_hi[src, :], t_lo, preferred_element_type=F32)
        )
        y_ref[dst, :] += part


def round_filtered(y_ref, f_even, f_odd):
    for mb in range(BLOCKS):
        f_even[mb * 16 : mb * 16 + 16, :] = y_ref[mb * 32 : mb * 32 + 16, :].astype(BF16)
        f_odd[mb * 16 : mb * 16 + 16, :] = y_ref[mb * 32 + 16 : mb * 32 + 32, :].astype(BF16)


def pick_columns(f_ref, index):
    low = jnp.bitwise_and(index, SUB - 1)
    high = lax.shift_right_logical(index, 8)
    row = lax.broadcasted_iota(I32, (SUB, TILE), 0)
    hot = one_hot(row == low)
    wide = jnp.dot(f_ref[...], hot, preferred_element_type=F32)
    high16 = jnp.broadcast_to(high, (ROWS, TILE))
    got = wide[:ROWS]
    for mb in range(1, BLOCKS):
        got = jnp.where(high16 == mb, wide[mb * ROWS : (mb + 1) * ROWS], got)
    return got


def interpolate_columns(at, f_even, f_odd, c_ref, b_ref, w_ref):
    where = pl.ds(at, TILE)
    column = c_ref[:, where]
    frac = b_ref[:, where]
    weight = w_ref[:, where]
    odd = jnp.bitwise_and(column, 1) == 1
    even_weight = jnp.where(odd, frac, 1.0 - frac) * weight
    odd_weight = jnp.where(odd, 1.0 - frac, frac) * weight
    even_part = pick_columns(f_even, lax.shift_right_logical(column + 1, 1))
    odd_part = pick_columns(f_odd, lax.shift_right_logical(column, 1))
    return even_part * even_weight + odd_part * odd_weight


def pair_halves(read, k, core):
    first = core * OUT_VOX + k * 64
    second = first + 2 * OUT_VOX
    return jnp.concatenate([read(first), read(second)], axis=1)


def deal_columns(src, dst):
    for s in range(SLABS):
        dst[:, s * 128 : (s + 1) * 128] = pair_halves(
            lambda at: src[:, at : at + 64], s // 2, s % 2
        )


def deal_rows(slab, start_v, rows_v, frac_v, s_send):
    lane = lax.broadcasted_iota(I32, (1, SLABS), 1)
    first_row = BAND * jnp.sum(jnp.where(lane == slab, start_v[...], 0), axis=1, keepdims=True)
    for q in range(OWNERS):
        lanes = slice(q * OUT_VOX, (q + 1) * OUT_VOX)
        position = (rows_v[:, lanes] + first_row).astype(F32) + frac_v[:, lanes]
        for k in range(16):
            half = slice((q // 2) * 64, (q // 2) * 64 + 64)
            s_send[2 * k + q % 2, :, half] = position[:, k * 64 : k * 64 + 64]


def transpose_rows(s_recv, st_ref):
    for zh in range(2):
        for th in range(2):
            block = s_recv[th * 16 : th * 16 + 16, zh * 8 : zh * 8 + 8, :].reshape(128, 128)
            at = (zh * 2 + th) * 128
            st_ref[:, at : at + 128] = block.T


def make_tables(h_recv):
    return [h_recv[g * 8 : (g + 1) * 8].reshape(128, 128).astype(F32).T for g in range(4)]


def look_up(position, tables, v):
    row = position.astype(I32)
    frac = position - row.astype(F32)
    values = []
    for r in (row, jnp.minimum(row + 1, DET - 1)):
        lane = (
            jnp.bitwise_and(lax.shift_right_logical(r, 2), 7) * 16
            + lax.shift_right_logical(r, 7) * 4
            + jnp.bitwise_and(r, 3)
        )
        which = jnp.bitwise_and(lax.shift_right_logical(r, 5), 3)
        got = None
        for k in range(4):
            part = jnp.take_along_axis(
                tables[k][v * 8 : v * 8 + 8], lane, axis=1, mode="promise_in_bounds"
            )
            got = part if got is None else jnp.where(which == k, part, got)
        values.append(got)
    return (1.0 - frac) * values[0] + frac * values[1]


def look_up_half(th, st_ref, tables, o_send):
    found = []
    for zh in range(2):
        at = (zh * 2 + th) * 128
        found.append(
            [look_up(st_ref[v * 8 : v * 8 + 8, at : at + 128], tables, v) for v in range(16)]
        )
    for e in range(2):
        stack = jnp.concatenate(found[0][e * 8 : e * 8 + 8] + found[1][e * 8 : e * 8 + 8], axis=0)
        o_send[e, th * 16 : th * 16 + 16] = stack.T.reshape(16, 8, 128)


def sum_angles(o_recv, out_ref):
    for m in range(8):
        total = []
        for k in (2 * m, 2 * m + 1):
            total.append(o_recv[k] + o_recv[16 + k] + o_recv[32 + k] + o_recv[48 + k])
        lanes = slice(m * 128, (m + 1) * 128)
        for zh in range(2):
            half = slice(zh * 64, zh * 64 + 64)
            out_ref[zh * 8 : zh * 8 + 8, lanes] = jnp.concatenate(
                [total[0][:, half], total[1][:, half]], axis=1
            )


def kernel(
    x_hbm, start_hbm, rows_hbm, frac_hbm, col_hbm, colf_hbm, dist_hbm, out_ref,
    x_v, start_v, rows_v, frac_v, col_v, colf_v, dist_v,
    col_d, colf_d, dist_d,
    toep_hi, toep_lo, xs_hi, xs_lo, z_hi, z_lo, y_ref, f_even, f_odd,
    s_send, s_recv, h_send, h_recv, o_send, o_recv, st_ref,
    in_sem, s_ssem, s_rsem, h_ssem, h_rsem, o_ssem, o_rsem, plane_sem,
):
    angle = lax.axis_index("angle")
    slab = lax.axis_index("slab")
    chip = slab // 2
    core = slab % 2
    at_home = angle % 2 == core

    barrier = pltpu.get_barrier_semaphore()

    def greet_slab(o, carry):
        pl.semaphore_signal(
            barrier, inc=1, device_id=(angle, lax.rem(slab + o, SLABS)), device_id_type=MESH
        )
        return carry

    lax.fori_loop(1, SLABS, greet_slab, 0)
    for o in range(1, ANGLES):
        pl.semaphore_signal(
            barrier, inc=1, device_id=(lax.rem(angle + o, ANGLES), slab), device_id_type=MESH
        )

    loads = [
        pltpu.make_async_copy(src, dst, in_sem.at[i])
        for i, (src, dst) in enumerate(
            (
                (x_hbm, x_v),
                (start_hbm, start_v),
                (rows_hbm, rows_v),
                (frac_hbm, frac_v),
                (col_hbm, col_v),
                (colf_hbm, colf_v),
                (dist_hbm, dist_v),
            )
        )
    ]
    for load in loads:
        load.start()

    make_toeplitz(toep_hi, toep_lo)
    for load in loads:
        load.wait()
    deal_rows(slab, start_v, rows_v, frac_v, s_send)
    for src, dst in ((col_v, col_d), (colf_v, colf_d), (dist_v, dist_d)):
        deal_columns(src, dst)
    load_weighted(slab, x_v, xs_hi, xs_lo)
    split_parity(xs_hi, xs_lo, z_hi, z_lo, y_ref)
    convolve(toep_hi, toep_lo, z_hi, z_lo, y_ref)
    round_filtered(y_ref, f_even, f_odd)

    pl.semaphore_wait(barrier, SLABS - 1 + ANGLES - 1)
    for o in range(1, ANGLES):
        pl.semaphore_signal(
            plane_sem, inc=1, device_id=(lax.rem(angle + o, ANGLES), slab), device_id_type=MESH
        )

    def send_rows(o, carry):
        peer = lax.rem(slab + o, SLABS)
        pltpu.make_async_remote_copy(
            src_ref=s_send.at[peer], dst_ref=s_recv.at[slab],
            send_sem=s_ssem, recv_sem=s_rsem,
            device_id=(angle, peer), device_id_type=MESH,
        ).start()
        return carry

    lax.fori_loop(1, SLABS, send_rows, 0)
    s_recv[slab] = s_send[slab]

    def columns(i, carry):
        j = i // 2
        turn = lax.rem(slab // 8 + 2 + j + (j // 2) * (5 - 2 * j), 4)
        tile = turn * 2 + lax.rem(slab // 4 + 1 + i, 2)
        at = pl.multiple_of(tile * TILE, TILE)
        value = interpolate_columns(at, f_even, f_odd, col_d, colf_d, dist_d).astype(BF16)
        for j in range(TILE // 128):
            peer = tile * (TILE // 128) + j
            h_send[peer] = value[:, j * 128 : (j + 1) * 128]

            @pl.when(peer != slab)
            def _():
                pltpu.make_async_remote_copy(
                    src_ref=h_send.at[peer], dst_ref=h_recv.at[slab],
                    send_sem=h_ssem, recv_sem=h_rsem,
                    device_id=(angle, peer), device_id_type=MESH,
                ).start()

        return carry

    lax.fori_loop(0, VOX // TILE, columns, 0)
    h_recv[slab] = h_send[slab]

    def wait_bytes(ref, count, sem):
        pltpu.make_async_copy(ref.at[pl.ds(0, count)], ref.at[pl.ds(0, count)], sem).wait()

    wait_bytes(s_recv, SLABS - 1, s_rsem)
    transpose_rows(s_recv, st_ref)
    wait_bytes(h_recv, SLABS - 1, h_rsem)
    tables = make_tables(h_recv)
    pl.semaphore_wait(plane_sem, ANGLES - 1)

    slot = angle * 16 + chip
    for th in range(2):
        look_up_half(th, st_ref, tables, o_send)

        def send_planes(o, carry):
            t = th * 16 + lax.rem(slab + o, 16)
            for e in range(2):
                owner = core + 2 * e

                @pl.when(jnp.logical_not(jnp.logical_and(owner == angle, t == slab)))
                def _():
                    pltpu.make_async_remote_copy(
                        src_ref=o_send.at[e, t], dst_ref=o_recv.at[slot],
                        send_sem=o_ssem, recv_sem=o_rsem,
                        device_id=(owner, t), device_id_type=MESH,
                    ).start()

            return carry

        lax.fori_loop(0, 16, send_planes, 0)

    @pl.when(at_home)
    def _():
        o_recv[slot] = o_send[angle // 2, slab]
        wait_bytes(o_recv, 63, o_rsem)

    @pl.when(jnp.logical_not(at_home))
    def _():
        wait_bytes(o_recv, 64, o_rsem)

    sum_angles(o_recv, out_ref)

    wait_bytes(s_send, SLABS - 1, s_ssem)
    wait_bytes(h_send, SLABS - 1, h_ssem)

    @pl.when(at_home)
    def _():
        wait_bytes(o_recv, 63, o_ssem)

    @pl.when(jnp.logical_not(at_home))
    def _():
        wait_bytes(o_recv, 64, o_ssem)


SCRATCH = [
    pltpu.VMEM((BANDS, BAND, COLS), F32),
    pltpu.VMEM((1, SLABS), I32),
    pltpu.VMEM((PLANES, VOX), I32),
    pltpu.VMEM((PLANES, VOX), F32),
    pltpu.VMEM((1, VOX), I32),
    pltpu.VMEM((1, VOX), F32),
    pltpu.VMEM((1, VOX), F32),
    pltpu.VMEM((1, VOX), I32),
    pltpu.VMEM((1, VOX), F32),
    pltpu.VMEM((1, VOX), F32),
    pltpu.VMEM((128, TOEP_WIDTH), BF16),
    pltpu.VMEM((128, TOEP_WIDTH), BF16),
    pltpu.VMEM((2 * SUB + ROWS, SUB), BF16),
    pltpu.VMEM((2 * SUB + ROWS, SUB), BF16),
    pltpu.VMEM((2 * SUB, SUB), BF16),
    pltpu.VMEM((2 * SUB, SUB), BF16),
    pltpu.VMEM((2 * SUB, SUB), F32),
    pltpu.VMEM((SUB, SUB), BF16),
    pltpu.VMEM((SUB, SUB), BF16),
    pltpu.VMEM((SLABS, PLANES, 128), F32),
    pltpu.VMEM((SLABS, PLANES, 128), F32),
    pltpu.VMEM((SLABS, ROWS, 128), BF16),
    pltpu.VMEM((SLABS, ROWS, 128), BF16),
    pltpu.VMEM((2, SLABS, 8, 128), F32),
    pltpu.VMEM((2 * SLABS, 8, 128), F32),
    pltpu.VMEM((128, SLABS * PLANES), F32),
    pltpu.SemaphoreType.DMA((7,)),
    pltpu.SemaphoreType.DMA,
    pltpu.SemaphoreType.DMA,
    pltpu.SemaphoreType.DMA,
    pltpu.SemaphoreType.DMA,
    pltpu.SemaphoreType.DMA,
    pltpu.SemaphoreType.DMA,
    pltpu.SemaphoreType.REGULAR,
]


def body(projections, band_start, row_index, row_frac, col_index, col_frac, distance_weight):
    call = pl.pallas_call(
        kernel,
        out_shape=jax.ShapeDtypeStruct((PLANES, OUT_VOX), F32),
        in_specs=[pl.BlockSpec(memory_space=pltpu.HBM)] * 7,
        out_specs=pl.BlockSpec(memory_space=pltpu.VMEM),
        scratch_shapes=SCRATCH,
        compiler_params=pltpu.CompilerParams(
            collective_id=0, has_side_effects=True, vmem_limit_bytes=40 * 1024 * 1024
        ),
        cost_estimate=pl.CostEstimate(
            flops=6 * 10**9, bytes_accessed=2 * 10**6, transcendentals=0
        ),
    )
    return call(
        projections.reshape(BANDS, BAND, COLS),
        band_start,
        row_index.reshape(PLANES, VOX),
        row_frac.reshape(PLANES, VOX),
        col_index,
        col_frac,
        distance_weight,
    )


def solution(mesh):
    in_specs = (
        P("angle", None, "slab", None, None),
        P("angle", None),
        P("angle", "slab", None),
        P("angle", "slab", None),
        P("angle", None),
        P("angle", None),
        P("angle", None),
    )
    out_specs = P("slab", "angle")
    return jax.shard_map(body, mesh=mesh, in_specs=in_specs, out_specs=out_specs, check_vma=False)
```

```python
import math

import jax
import jax.numpy as jnp
from jax import lax
from jax.experimental import pallas as pl
from jax.experimental.pallas import tpu as pltpu
from jax.sharding import PartitionSpec as P

F32 = jnp.float32
BF16 = jnp.bfloat16
I32 = jnp.int32
MESH = pl.DeviceIdType.MESH

ANGLES = 4
OWNERS = 4
SLABS = 32
BANDS = 4
BAND = 4
ROWS = 16
COLS = 8192
DET = 512
PLANES = 16
VOX = 4096
OUT_VOX = 1024
SUB = 256
BLOCKS = 16
HALF = COLS // 2
TOEP_LO = -(BLOCKS - 1) * SUB - 128
TOEP_WIDTH = (2 * BLOCKS - 1) * SUB + 128
TILE = 512
FAR_FIRST = sorted(
    ((dy, dz, dc) for dy in range(4) for dz in range(4) for dc in range(2)),
    key=lambda at: (-min(at[0], 4 - at[0]) - min(at[1], 4 - at[1]), -at[2], at[0], at[1]),
)
TILE_ORDER = ((2, 1), (2, 0), (1, 1), (3, 1), (1, 0), (3, 0), (0, 1), (0, 0))


def split_hi_lo(value):
    high = value.astype(BF16)
    low = (value - high.astype(F32)).astype(BF16)
    return high, low


def ramp_odd(offset):
    step = (2 * offset - 1).astype(F32)
    return (-1.0 / math.pi**2) / (step * step)


def make_toeplitz(toep):
    lane = lax.broadcasted_iota(I32, (128, 128), 1)
    sub = lax.broadcasted_iota(I32, (128, 128), 0)
    base = (2 * (lane - sub + TOEP_LO) - 1).astype(F32)

    def one(j, carry):
        for i in range(3):
            tile = j * 3 + i
            step = base + 256.0 * tile.astype(F32)
            square = step * step
            guess = pltpu.reciprocal(square, approx=True)
            guess = guess * (2.0 - square * guess)
            high, low = split_hi_lo(guess * (-1.0 / math.pi**2))
            where = pl.ds(pl.multiple_of(tile * 128, 128), 128)
            toep[0, :, where] = high
            toep[1, :, where] = low
        return carry

    lax.fori_loop(0, TOEP_WIDTH // 384, one, 0)


def make_hot(n, col_d, hot_even, hot_odd):
    lanes = pl.ds(pl.multiple_of(n * SUB, SUB), SUB)
    column = col_d[:, lanes]
    row = lax.broadcasted_iota(I32, (SUB, SUB), 0).astype(F32).astype(BF16)
    one = jnp.ones((SUB, SUB), BF16)
    zero = jnp.zeros((SUB, SUB), BF16)
    for hot, index in (
        (hot_even, lax.shift_right_logical(column + 1, 1)),
        (hot_odd, lax.shift_right_logical(column, 1)),
    ):
        low = jnp.bitwise_and(index, SUB - 1).astype(F32).astype(BF16)
        hot[:, lanes] = jnp.where(row == low, one, zero)


def load_weighted(slab, x_ref, xs_hi, xs_lo):
    scale = 2.0 * COLS
    row = lax.broadcasted_iota(I32, (ROWS, SUB), 0)
    lane = lax.broadcasted_iota(I32, (ROWS, SUB), 1)
    det = ((row // BAND) * SLABS + slab) * BAND + row % BAND
    down = det.astype(F32) - (DET - 1) / 2.0
    rest = scale * scale + down * down
    for kb in range(COLS // SUB):
        across = (lane + kb * SUB).astype(F32) - (COLS - 1) / 2.0
        raw = jnp.concatenate(
            [x_ref[b, :, kb * SUB : (kb + 1) * SUB] for b in range(BANDS)], axis=0
        )
        high, low = split_hi_lo(raw * (scale / jnp.sqrt(rest + across * across)))
        xs_hi[kb * ROWS : (kb + 1) * ROWS, :] = high
        xs_lo[kb * ROWS : (kb + 1) * ROWS, :] = low
    xs_hi[2 * SUB :, :] = jnp.zeros((ROWS, SUB), BF16)
    xs_lo[2 * SUB :, :] = jnp.zeros((ROWS, SUB), BF16)


def one_hot(mask):
    return jnp.where(mask, 1.0, 0.0).astype(BF16)


def split_parity(xs_hi, xs_lo, z_ref, y_ref):
    k = lax.broadcasted_iota(I32, (SUB, SUB), 0)
    n = lax.broadcasted_iota(I32, (SUB, SUB), 1)
    even_odd = one_hot(k == jnp.where(n < 128, 2 * n, 2 * n - 255))
    k2 = lax.broadcasted_iota(I32, (2 * SUB, 128), 0)
    n2 = lax.broadcasted_iota(I32, (2 * SUB, 128), 1)
    later = one_hot(k2 == 2 * n2 + 2)
    first = None
    quarter = None
    for part, xs in enumerate((xs_hi, xs_lo)):
        here = xs[: 2 * SUB, :]
        both = jnp.concatenate([here, xs[ROWS : 2 * SUB + ROWS, :]], axis=1)
        eo = jnp.dot(here, even_odd, preferred_element_type=F32)
        es = jnp.dot(both, later, preferred_element_type=F32).astype(BF16)
        eo_b = eo[:, 128:].astype(BF16)
        for kb in range(2 * BLOCKS):
            mb, half = kb // 2, kb % 2
            lanes = slice(half * 128, half * 128 + 128)
            src = slice(kb * ROWS, (kb + 1) * ROWS)
            z_ref[part, mb * 32 : mb * 32 + 16, lanes] = eo_b[src]
            z_ref[part, mb * 32 + 16 : mb * 32 + 32, lanes] = es[src]
        quarter = eo if quarter is None else quarter + eo
        first = eo[:ROWS, 0:1] if first is None else first + eo[:ROWS, 0:1]
    quarter = quarter * 0.25
    lane = lax.broadcasted_iota(I32, (ROWS, 128), 1)
    for kb in range(2 * BLOCKS):
        mb, half = kb // 2, kb % 2
        lanes = slice(half * 128, half * 128 + 128)
        src = slice(kb * ROWS, (kb + 1) * ROWS)
        y_ref[mb * 32 : mb * 32 + 16, lanes] = quarter[src, :128]
        edge = first * ramp_odd(lane + (kb * 128 + 1))
        y_ref[mb * 32 + 16 : mb * 32 + 32, lanes] = quarter[src, 128:] + edge


def convolve(col_d, toep, hot_even, hot_odd, z_ref, y_ref):
    def one_pass(turn, carry):
        z_at = turn % 2
        t_at = turn // 2
        for n in range(2 * BLOCKS - 1):
            d = n - (BLOCKS - 1)
            at = n * SUB + 128
            count = (BLOCKS - abs(d)) * 32
            src = slice(max(0, -d) * 32, max(0, -d) * 32 + count)
            dst = slice(max(0, d) * 32, max(0, d) * 32 + count)
            table = jnp.concatenate(
                [toep[t_at, :, at : at + SUB], toep[t_at, :, at - 128 : at + 128]], axis=0
            )
            y_ref[dst, :] += jnp.dot(z_ref[z_at, src, :], table, preferred_element_type=F32)
            if n % 5 == 2:
                make_hot(jnp.minimum(turn * 6 + n // 5, VOX // SUB - 1), col_d, hot_even, hot_odd)
        return carry

    lax.fori_loop(0, 3, one_pass, 0)


def round_filtered(y_ref, f_even, f_odd):
    for mb in range(BLOCKS):
        f_even[mb * 16 : mb * 16 + 16, :] = y_ref[mb * 32 : mb * 32 + 16, :].astype(BF16)
        f_odd[mb * 16 : mb * 16 + 16, :] = y_ref[mb * 32 + 16 : mb * 32 + 32, :].astype(BF16)


def pick_columns(f_ref, hot, index):
    high16 = jnp.broadcast_to(lax.shift_right_logical(index, 8), (ROWS, TILE))
    wide = jnp.dot(f_ref[...], hot, preferred_element_type=F32)
    got = wide[:ROWS]
    for mb in range(1, BLOCKS):
        got = jnp.where(high16 == mb, wide[mb * ROWS : (mb + 1) * ROWS], got)
    return got


def interpolate_columns(at, f_even, f_odd, hot_even, hot_odd, c_ref, b_ref, w_ref):
    where = pl.ds(at, TILE)
    column = c_ref[:, where]
    frac = b_ref[:, where]
    weight = w_ref[:, where]
    odd = jnp.bitwise_and(column, 1) == 1
    even_weight = jnp.where(odd, frac, 1.0 - frac) * weight
    odd_weight = jnp.where(odd, 1.0 - frac, frac) * weight
    even_part = pick_columns(f_even, hot_even[:, where], lax.shift_right_logical(column + 1, 1))
    odd_part = pick_columns(f_odd, hot_odd[:, where], lax.shift_right_logical(column, 1))
    return even_part * even_weight + odd_part * odd_weight


def pair_halves(read, k, core):
    first = core * OUT_VOX + k * 64
    second = first + 2 * OUT_VOX
    return jnp.concatenate([read(first), read(second)], axis=1)


def deal_columns(src, dst):
    for s in range(SLABS):
        dst[:, s * 128 : (s + 1) * 128] = pair_halves(
            lambda at: src[:, at : at + 64], s // 2, s % 2
        )


def deal_rows(slab, start_v, rows_v, frac_v, s_send):
    lane = lax.broadcasted_iota(I32, (1, SLABS), 1)
    first_row = BAND * jnp.sum(jnp.where(lane == slab, start_v[...], 0), axis=1, keepdims=True)
    for q in range(OWNERS):
        lanes = slice(q * OUT_VOX, (q + 1) * OUT_VOX)
        position = (rows_v[:, lanes] + first_row).astype(F32) + frac_v[:, lanes]
        for k in range(16):
            half = slice((q // 2) * 64, (q // 2) * 64 + 64)
            s_send[2 * k + q % 2, :, half] = position[:, k * 64 : k * 64 + 64]


def transpose_rows(s_recv, st_ref):
    for zh in range(2):
        for th in range(2):
            block = s_recv[th * 16 : th * 16 + 16, zh * 8 : zh * 8 + 8, :].reshape(128, 128)
            at = (zh * 2 + th) * 128
            st_ref[:, at : at + 128] = block.T


def make_tables(h_recv):
    return [h_recv[g * 8 : (g + 1) * 8].reshape(128, 128).astype(F32).T for g in range(4)]


def look_up(position, tables, v):
    row = position.astype(I32)
    frac = position - row.astype(F32)
    values = []
    for r in (row, jnp.minimum(row + 1, DET - 1)):
        lane = (
            jnp.bitwise_and(lax.shift_right_logical(r, 2), 7) * 16
            + lax.shift_right_logical(r, 7) * 4
            + jnp.bitwise_and(r, 3)
        )
        which = jnp.bitwise_and(lax.shift_right_logical(r, 5), 3)
        got = None
        for k in range(4):
            part = jnp.take_along_axis(
                tables[k][v * 8 : v * 8 + 8], lane, axis=1, mode="promise_in_bounds"
            )
            got = part if got is None else jnp.where(which == k, part, got)
        values.append(got)
    return (1.0 - frac) * values[0] + frac * values[1]


def look_up_half(th, st_ref, tables, o_send):
    found = []
    for zh in range(2):
        at = (zh * 2 + th) * 128
        found.append(
            [look_up(st_ref[v * 8 : v * 8 + 8, at : at + 128], tables, v) for v in range(16)]
        )
    for e in range(2):
        stack = jnp.concatenate(found[0][e * 8 : e * 8 + 8] + found[1][e * 8 : e * 8 + 8], axis=0)
        o_send[e, th * 16 : th * 16 + 16] = stack.T.reshape(16, 8, 128)


def sum_angles(o_recv, out_ref):
    for m in range(8):
        total = []
        for k in (2 * m, 2 * m + 1):
            total.append(o_recv[k] + o_recv[16 + k] + o_recv[32 + k] + o_recv[48 + k])
        lanes = slice(m * 128, (m + 1) * 128)
        for zh in range(2):
            half = slice(zh * 64, zh * 64 + 64)
            out_ref[zh * 8 : zh * 8 + 8, lanes] = jnp.concatenate(
                [total[0][:, half], total[1][:, half]], axis=1
            )


def kernel(
    x_hbm, start_hbm, rows_hbm, frac_hbm, col_hbm, colf_hbm, dist_hbm, out_ref,
    x_v, start_v, rows_v, frac_v, col_v, colf_v, dist_v,
    col_d, colf_d, dist_d,
    toep, hot_even, hot_odd, xs_hi, xs_lo, z_ref, y_ref, f_even, f_odd,
    s_send, s_recv, h_send, h_recv, o_send, o_recv, st_ref,
    in_sem, s_ssem, s_rsem, h_ssem, h_rsem, o_ssem, o_rsem, plane_sem,
):
    angle = lax.axis_index("angle")
    slab = lax.axis_index("slab")
    chip = slab // 2
    core = slab % 2
    at_home = angle % 2 == core

    ys = [lax.rem(slab // 8 + dy, 4) * 8 for dy in range(4)]
    zs = [lax.rem(chip + dz, 4) * 2 for dz in range(4)]
    cores = (core, 1 - core)

    def far_first(o):
        dy, dz, dc = FAR_FIRST[o]
        return ys[dy] + zs[dz] + cores[dc]

    loads = [
        pltpu.make_async_copy(src, dst, in_sem.at[i])
        for i, (src, dst) in enumerate(
            (
                (x_hbm, x_v),
                (col_hbm, col_v),
                (colf_hbm, colf_v),
                (dist_hbm, dist_v),
                (start_hbm, start_v),
                (rows_hbm, rows_v),
                (frac_hbm, frac_v),
            )
        )
    ]
    for load in loads:
        load.start()

    barrier = pltpu.get_barrier_semaphore()

    def greet(o, carry):
        pl.semaphore_signal(
            barrier, inc=1, device_id=(angle, far_first(o)), device_id_type=MESH
        )
        return carry

    for o in range(SLABS - 1):
        greet(o, 0)
    for o in range(1, ANGLES):
        pl.semaphore_signal(
            barrier, inc=1, device_id=(lax.rem(angle + o, ANGLES), slab), device_id_type=MESH
        )

    make_toeplitz(toep)
    for load in loads:
        load.wait()
    for src, dst in ((col_v, col_d), (colf_v, colf_d), (dist_v, dist_d)):
        deal_columns(src, dst)
    load_weighted(slab, x_v, xs_hi, xs_lo)
    split_parity(xs_hi, xs_lo, z_ref, y_ref)
    deal_rows(slab, start_v, rows_v, frac_v, s_send)

    pl.semaphore_wait(barrier, SLABS - 1 + ANGLES - 1)
    for o in range(1, ANGLES):
        pl.semaphore_signal(
            plane_sem, inc=1, device_id=(lax.rem(angle + o, ANGLES), slab), device_id_type=MESH
        )

    def send(src, dst, send_sem, recv_sem, to_angle, to_slab):
        pltpu.make_async_remote_copy(
            src_ref=src, dst_ref=dst, send_sem=send_sem, recv_sem=recv_sem,
            device_id=(to_angle, to_slab), device_id_type=MESH,
        ).start()

    def send_rows(o, carry):
        peer = far_first(o)
        send(s_send.at[peer], s_recv.at[slab], s_ssem, s_rsem, angle, peer)
        return carry

    for o in range(SLABS - 1):
        send_rows(o, 0)
    s_recv[slab] = s_send[slab]

    convolve(col_d, toep, hot_even, hot_odd, z_ref, y_ref)
    round_filtered(y_ref, f_even, f_odd)

    for i, (dy, dz) in enumerate(TILE_ORDER):
        tile = lax.rem(slab // 8 + dy, 4) * 2 + lax.rem(slab // 4 + dz, 2)
        at = pl.multiple_of(tile * TILE, TILE)
        value = interpolate_columns(
            at, f_even, f_odd, hot_even, hot_odd, col_d, colf_d, dist_d
        ).astype(BF16)
        for j in range(4):
            h_send[tile * 4 + j] = value[:, j * 128 : (j + 1) * 128]
        for j in range(4):
            peer = tile * 4 + lax.rem(slab + j, 4)
            if i < len(TILE_ORDER) - 1 or j > 0:
                send(h_send.at[peer], h_recv.at[slab], h_ssem, h_rsem, angle, peer)
    h_recv[slab] = h_send[slab]

    def wait_bytes(ref, count, sem):
        pltpu.make_async_copy(ref.at[pl.ds(0, count)], ref.at[pl.ds(0, count)], sem).wait()

    wait_bytes(s_recv, SLABS - 1, s_rsem)
    transpose_rows(s_recv, st_ref)
    pl.semaphore_wait(plane_sem, ANGLES - 1)
    wait_bytes(h_recv, SLABS - 1, h_rsem)
    tables = make_tables(h_recv)
    for th in range(2):
        look_up_half(th, st_ref, tables, o_send)

    slot = angle * 16 + chip

    def send_planes(o, carry):
        t = far_first(o)
        for e in range(2):
            send(o_send.at[e, t], o_recv.at[slot], o_ssem, o_rsem, core + 2 * e, t)
        return carry

    for o in range(SLABS - 1):
        send_planes(o, 0)
    for e in range(2):

        @pl.when(core + 2 * e != angle)
        def _():
            send(o_send.at[e, slab], o_recv.at[slot], o_ssem, o_rsem, core + 2 * e, slab)

    @pl.when(at_home)
    def _():
        o_recv[slot] = o_send[angle // 2, slab]
        wait_bytes(o_recv, 63, o_rsem)

    @pl.when(jnp.logical_not(at_home))
    def _():
        wait_bytes(o_recv, 64, o_rsem)

    sum_angles(o_recv, out_ref)

    wait_bytes(s_send, SLABS - 1, s_ssem)
    wait_bytes(h_send, SLABS - 1, h_ssem)

    @pl.when(at_home)
    def _():
        wait_bytes(o_recv, 63, o_ssem)

    @pl.when(jnp.logical_not(at_home))
    def _():
        wait_bytes(o_recv, 64, o_ssem)


SCRATCH = [
    pltpu.VMEM((BANDS, BAND, COLS), F32),
    pltpu.VMEM((1, SLABS), I32),
    pltpu.VMEM((PLANES, VOX), I32),
    pltpu.VMEM((PLANES, VOX), F32),
    pltpu.VMEM((1, VOX), I32),
    pltpu.VMEM((1, VOX), F32),
    pltpu.VMEM((1, VOX), F32),
    pltpu.VMEM((1, VOX), I32),
    pltpu.VMEM((1, VOX), F32),
    pltpu.VMEM((1, VOX), F32),
    pltpu.VMEM((2, 128, TOEP_WIDTH), BF16),
    pltpu.VMEM((SUB, VOX), BF16),
    pltpu.VMEM((SUB, VOX), BF16),
    pltpu.VMEM((2 * SUB + ROWS, SUB), BF16),
    pltpu.VMEM((2 * SUB + ROWS, SUB), BF16),
    pltpu.VMEM((2, 2 * SUB, SUB), BF16),
    pltpu.VMEM((2 * SUB, SUB), F32),
    pltpu.VMEM((SUB, SUB), BF16),
    pltpu.VMEM((SUB, SUB), BF16),
    pltpu.VMEM((SLABS, PLANES, 128), F32),
    pltpu.VMEM((SLABS, PLANES, 128), F32),
    pltpu.VMEM((SLABS, ROWS, 128), BF16),
    pltpu.VMEM((SLABS, ROWS, 128), BF16),
    pltpu.VMEM((2, SLABS, 8, 128), F32),
    pltpu.VMEM((2 * SLABS, 8, 128), F32),
    pltpu.VMEM((128, SLABS * PLANES), F32),
    pltpu.SemaphoreType.DMA((7,)),
    pltpu.SemaphoreType.DMA,
    pltpu.SemaphoreType.DMA,
    pltpu.SemaphoreType.DMA,
    pltpu.SemaphoreType.DMA,
    pltpu.SemaphoreType.DMA,
    pltpu.SemaphoreType.DMA,
    pltpu.SemaphoreType.REGULAR,
]


def body(projections, band_start, row_index, row_frac, col_index, col_frac, distance_weight):
    call = pl.pallas_call(
        kernel,
        out_shape=jax.ShapeDtypeStruct((PLANES, OUT_VOX), F32),
        in_specs=[pl.BlockSpec(memory_space=pltpu.HBM)] * 7,
        out_specs=pl.BlockSpec(memory_space=pltpu.VMEM),
        scratch_shapes=SCRATCH,
        compiler_params=pltpu.CompilerParams(
            collective_id=0, has_side_effects=True, vmem_limit_bytes=40 * 1024 * 1024
        ),
        cost_estimate=pl.CostEstimate(
            flops=6 * 10**9, bytes_accessed=2 * 10**6, transcendentals=0
        ),
    )
    operands = (
        projections.reshape(BANDS, BAND, COLS),
        band_start,
        row_index.reshape(PLANES, VOX),
        row_frac.reshape(PLANES, VOX),
        col_index,
        col_frac,
        distance_weight,
    )
    return call(*(pltpu.with_memory_space_constraint(value, pltpu.HBM) for value in operands))


def solution(mesh):
    in_specs = (
        P("angle", None, "slab", None, None),
        P("angle", None),
        P("angle", "slab", None),
        P("angle", "slab", None),
        P("angle", None),
        P("angle", None),
        P("angle", None),
    )
    out_specs = P("slab", "angle")
    return jax.shard_map(body, mesh=mesh, in_specs=in_specs, out_specs=out_specs, check_vma=False)
```

```python
import math

import jax
import jax.numpy as jnp
from jax import lax
from jax.experimental import pallas as pl
from jax.experimental.pallas import tpu as pltpu
from jax.sharding import PartitionSpec as P

F32 = jnp.float32
BF16 = jnp.bfloat16
I32 = jnp.int32
MESH = pl.DeviceIdType.MESH

ANGLES = 4
OWNERS = 4
SLABS = 32
BANDS = 4
BAND = 4
ROWS = 16
COLS = 8192
DET = 512
PLANES = 16
VOX = 4096
OUT_VOX = 1024
SUB = 256
BLOCKS = 16
HALF = COLS // 2
TOEP_LO = -(BLOCKS - 1) * SUB - 128
TOEP_WIDTH = (2 * BLOCKS - 1) * SUB + 128
NEAR = 2
NEAR_LO = -NEAR * SUB - 128
NEAR_WIDTH = (2 * NEAR + 1) * SUB + 128
TILE = 512
FAR_CHIPS = sorted(
    ((dy, dz) for dy in range(4) for dz in range(4) if dy + dz > 0),
    key=lambda at: (-min(at[0], 4 - at[0]) - min(at[1], 4 - at[1]), at),
)
FAR_LANE = [(2, 1), (2, 0), (1, 1), (1, 0), (3, 1), (3, 0), (0, 1), (0, 0)]


def split_hi_lo(value):
    high = value.astype(BF16)
    low = (value - high.astype(F32)).astype(BF16)
    return high, low


def ramp_odd(offset):
    step = (2 * offset - 1).astype(F32)
    return (-1.0 / math.pi**2) / (step * step)


def make_toeplitz(toep, toep_near):
    lane = lax.broadcasted_iota(I32, (128, 128), 1)
    sub = lax.broadcasted_iota(I32, (128, 128), 0)
    base = (2 * (lane - sub + TOEP_LO) - 1).astype(F32)
    skip = (NEAR_LO - TOEP_LO) // 128

    def value(tile):
        step = base + 256.0 * tile.astype(F32)
        square = step * step
        guess = pltpu.reciprocal(square, approx=True)
        return guess * (2.0 - square * guess) * (-1.0 / math.pi**2)

    def one(j, carry):
        for i in range(3):
            tile = j * 3 + i
            toep[:, pl.ds(pl.multiple_of(tile * 128, 128), 128)] = value(tile).astype(BF16)
        return carry

    def near(j, carry):
        where = pl.ds(pl.multiple_of(j * 128, 128), 128)
        high, low = split_hi_lo(value(j + skip))
        toep_near[0, :, where] = high
        toep_near[1, :, where] = low
        return carry

    lax.fori_loop(0, TOEP_WIDTH // 384, one, 0)
    lax.fori_loop(0, NEAR_WIDTH // 128, near, 0)


def make_hot(n, col_d, hot_even, hot_odd):
    lanes = slice(n * SUB, (n + 1) * SUB)
    column = col_d[:, lanes]
    row = lax.broadcasted_iota(I32, (SUB, SUB), 0).astype(F32).astype(BF16)
    one = jnp.ones((SUB, SUB), BF16)
    zero = jnp.zeros((SUB, SUB), BF16)
    for hot, index in (
        (hot_even, lax.shift_right_logical(column + 1, 1)),
        (hot_odd, lax.shift_right_logical(column, 1)),
    ):
        low = jnp.bitwise_and(index, SUB - 1).astype(F32).astype(BF16)
        hot[:, lanes] = jnp.where(row == low, one, zero)


def load_weighted(slab, x_ref, xs_hi, xs_lo):
    scale = 2.0 * COLS
    row = lax.broadcasted_iota(I32, (ROWS, SUB), 0)
    lane = lax.broadcasted_iota(I32, (ROWS, SUB), 1)
    det = ((row // BAND) * SLABS + slab) * BAND + row % BAND
    down = det.astype(F32) - (DET - 1) / 2.0
    rest = scale * scale + down * down
    for kb in range(COLS // SUB):
        across = (lane + kb * SUB).astype(F32) - (COLS - 1) / 2.0
        raw = jnp.concatenate(
            [x_ref[b, :, kb * SUB : (kb + 1) * SUB] for b in range(BANDS)], axis=0
        )
        high, low = split_hi_lo(raw * (scale / jnp.sqrt(rest + across * across)))
        xs_hi[kb * ROWS : (kb + 1) * ROWS, :] = high
        xs_lo[kb * ROWS : (kb + 1) * ROWS, :] = low
    xs_hi[2 * SUB :, :] = jnp.zeros((ROWS, SUB), BF16)
    xs_lo[2 * SUB :, :] = jnp.zeros((ROWS, SUB), BF16)


def one_hot(mask):
    return jnp.where(mask, 1.0, 0.0).astype(BF16)


def split_parity(xs_hi, xs_lo, z_ref, y_ref):
    k = lax.broadcasted_iota(I32, (SUB, SUB), 0)
    n = lax.broadcasted_iota(I32, (SUB, SUB), 1)
    even_odd = one_hot(k == jnp.where(n < 128, 2 * n, 2 * n - 255))
    k2 = lax.broadcasted_iota(I32, (2 * SUB, 128), 0)
    n2 = lax.broadcasted_iota(I32, (2 * SUB, 128), 1)
    later = one_hot(k2 == 2 * n2 + 2)
    first = None
    quarter = None
    for part, xs in enumerate((xs_hi, xs_lo)):
        here = xs[: 2 * SUB, :]
        both = jnp.concatenate([here, xs[ROWS : 2 * SUB + ROWS, :]], axis=1)
        eo = jnp.dot(here, even_odd, preferred_element_type=F32)
        es = jnp.dot(both, later, preferred_element_type=F32).astype(BF16)
        eo_b = eo[:, 128:].astype(BF16)
        for kb in range(2 * BLOCKS):
            mb, half = kb // 2, kb % 2
            lanes = slice(half * 128, half * 128 + 128)
            src = slice(kb * ROWS, (kb + 1) * ROWS)
            z_ref[part, mb * 32 : mb * 32 + 16, lanes] = eo_b[src]
            z_ref[part, mb * 32 + 16 : mb * 32 + 32, lanes] = es[src]
        quarter = eo if quarter is None else quarter + eo
        first = eo[:ROWS, 0:1] if first is None else first + eo[:ROWS, 0:1]
    quarter = quarter * 0.25
    lane = lax.broadcasted_iota(I32, (ROWS, 128), 1)
    for kb in range(2 * BLOCKS):
        mb, half = kb // 2, kb % 2
        lanes = slice(half * 128, half * 128 + 128)
        src = slice(kb * ROWS, (kb + 1) * ROWS)
        y_ref[mb * 32 : mb * 32 + 16, lanes] = quarter[src, :128]
        edge = first * ramp_odd(lane + (kb * 128 + 1))
        y_ref[mb * 32 + 16 : mb * 32 + 32, lanes] = quarter[src, 128:] + edge


def add_block(d, count, table, z_part, y_ref):
    src = max(0, -d) * 32
    dst = max(0, d) * 32
    y_ref[dst : dst + count, :] += jnp.dot(
        z_part[src : src + count, :], table, preferred_element_type=F32
    )


def two_rows(toep, at):
    return jnp.concatenate([toep[:, at : at + SUB], toep[:, at - 128 : at + 128]], axis=0)


def convolve_far(col_d, toep, hot_even, hot_odd, z_ref, y_ref):
    step = 0
    for d in range(-(BLOCKS - 1), BLOCKS):
        if abs(d) > NEAR:
            table = two_rows(toep, d * SUB - TOEP_LO)
            add_block(d, (BLOCKS - abs(d)) * 32, table, z_ref.at[0], y_ref)
            if step < VOX // SUB:
                make_hot(step, col_d, hot_even, hot_odd)
            step += 1


def convolve_near(toep_near, z_ref, y_ref):
    for d in range(-NEAR, NEAR + 1):
        for z_at, t_at in ((0, 0), (1, 0), (0, 1)):
            table = two_rows(toep_near.at[t_at], d * SUB - NEAR_LO)
            add_block(d, (BLOCKS - abs(d)) * 32, table, z_ref.at[z_at], y_ref)


def round_filtered(y_ref, f_even, f_odd):
    for mb in range(BLOCKS):
        f_even[mb * 16 : mb * 16 + 16, :] = y_ref[mb * 32 : mb * 32 + 16, :].astype(BF16)
        f_odd[mb * 16 : mb * 16 + 16, :] = y_ref[mb * 32 + 16 : mb * 32 + 32, :].astype(BF16)


def pick_columns(f_ref, hot, index):
    high16 = jnp.broadcast_to(lax.shift_right_logical(index, 8), (ROWS, TILE))
    wide = jnp.dot(f_ref[...], hot, preferred_element_type=F32)
    got = wide[:ROWS]
    for mb in range(1, BLOCKS):
        got = jnp.where(high16 == mb, wide[mb * ROWS : (mb + 1) * ROWS], got)
    return got


def interpolate_columns(at, f_even, f_odd, hot_even, hot_odd, c_ref, b_ref, w_ref):
    where = pl.ds(at, TILE)
    column = c_ref[:, where]
    frac = b_ref[:, where]
    weight = w_ref[:, where]
    odd = jnp.bitwise_and(column, 1) == 1
    even_weight = jnp.where(odd, frac, 1.0 - frac) * weight
    odd_weight = jnp.where(odd, 1.0 - frac, frac) * weight
    even_part = pick_columns(f_even, hot_even[:, where], lax.shift_right_logical(column + 1, 1))
    odd_part = pick_columns(f_odd, hot_odd[:, where], lax.shift_right_logical(column, 1))
    return even_part * even_weight + odd_part * odd_weight


def pair_halves(read, k, core):
    first = core * OUT_VOX + k * 64
    second = first + 2 * OUT_VOX
    return jnp.concatenate([read(first), read(second)], axis=1)


def deal_columns(src, dst):
    for s in range(SLABS):
        dst[:, s * 128 : (s + 1) * 128] = pair_halves(
            lambda at: src[:, at : at + 64], s // 2, s % 2
        )


def deal_rows(slab, start_v, rows_v, frac_v, s_send):
    lane = lax.broadcasted_iota(I32, (1, SLABS), 1)
    first_row = BAND * jnp.sum(jnp.where(lane == slab, start_v[...], 0), axis=1, keepdims=True)
    for q in range(OWNERS):
        lanes = slice(q * OUT_VOX, (q + 1) * OUT_VOX)
        position = (rows_v[:, lanes] + first_row).astype(F32) + frac_v[:, lanes]
        for k in range(16):
            half = slice((q // 2) * 64, (q // 2) * 64 + 64)
            s_send[2 * k + q % 2, :, half] = position[:, k * 64 : k * 64 + 64]


def transpose_rows(s_recv, st_ref):
    for zh in range(2):
        for th in range(2):
            block = s_recv[th * 16 : th * 16 + 16, zh * 8 : zh * 8 + 8, :].reshape(128, 128)
            at = (zh * 2 + th) * 128
            st_ref[:, at : at + 128] = block.T


def make_tables(h_recv):
    return [h_recv[g * 8 : (g + 1) * 8].reshape(128, 128).astype(F32).T for g in range(4)]


def look_up(position, tables, v):
    row = position.astype(I32)
    frac = position - row.astype(F32)
    values = []
    for r in (row, jnp.minimum(row + 1, DET - 1)):
        lane = (
            jnp.bitwise_and(lax.shift_right_logical(r, 2), 7) * 16
            + lax.shift_right_logical(r, 7) * 4
            + jnp.bitwise_and(r, 3)
        )
        which = jnp.bitwise_and(lax.shift_right_logical(r, 5), 3)
        got = None
        for k in range(4):
            part = jnp.take_along_axis(
                tables[k][v * 8 : v * 8 + 8], lane, axis=1, mode="promise_in_bounds"
            )
            got = part if got is None else jnp.where(which == k, part, got)
        values.append(got)
    return (1.0 - frac) * values[0] + frac * values[1]


def look_up_half(half, st_ref, tables, o_send):
    found = []
    for zh in range(2):
        lanes = pl.ds(pl.multiple_of((zh * 2 + half) * 128, 128), 128)
        found.append([look_up(st_ref[v * 8 : v * 8 + 8, lanes], tables, v) for v in range(16)])
    for e in range(2):
        stack = jnp.concatenate(found[0][e * 8 : e * 8 + 8] + found[1][e * 8 : e * 8 + 8], axis=0)
        o_send[e, pl.ds(half * 16, 16)] = stack.T.reshape(16, 8, 128)


def sum_angles(o_recv, out_ref):
    for m in range(8):
        total = []
        for k in (2 * m, 2 * m + 1):
            total.append(o_recv[k] + o_recv[16 + k] + o_recv[32 + k] + o_recv[48 + k])
        lanes = slice(m * 128, (m + 1) * 128)
        for zh in range(2):
            half = slice(zh * 64, zh * 64 + 64)
            out_ref[zh * 8 : zh * 8 + 8, lanes] = jnp.concatenate(
                [total[0][:, half], total[1][:, half]], axis=1
            )


def kernel(
    x_hbm, start_hbm, rows_hbm, frac_hbm, col_hbm, colf_hbm, dist_hbm, out_ref,
    x_v, start_v, rows_v, frac_v, col_v, colf_v, dist_v,
    col_d, colf_d, dist_d,
    toep, toep_near, hot_even, hot_odd, xs_hi, xs_lo, z_ref, y_ref, f_even, f_odd,
    s_send, s_recv, h_send, h_recv, o_send, o_recv, st_ref,
    in_sem, s_ssem, s_rsem, h_ssem, h_rsem, o_ssem, o_rsem, plane_sem,
):
    angle = lax.axis_index("angle")
    slab = lax.axis_index("slab")
    chip = slab // 2
    core = slab % 2
    at_home = angle % 2 == core

    ys = [lax.rem(slab // 8 + dy, 4) * 8 for dy in range(4)]
    zs = [lax.rem(chip + dz, 4) * 2 for dz in range(4)]
    cores = (core, 1 - core)

    loads = [
        pltpu.make_async_copy(src, dst, in_sem.at[i])
        for i, (src, dst) in enumerate(
            (
                (x_hbm, x_v),
                (col_hbm, col_v),
                (colf_hbm, colf_v),
                (dist_hbm, dist_v),
                (start_hbm, start_v),
                (rows_hbm, rows_v),
                (frac_hbm, frac_v),
            )
        )
    ]
    for load in loads:
        load.start()

    barrier = pltpu.get_barrier_semaphore()

    def greet(peer):
        pl.semaphore_signal(barrier, inc=1, device_id=(angle, peer), device_id_type=MESH)

    def greet_cores(turn, carry):
        same = turn * core + (1 - turn) * (1 - core)
        for dy, dz in FAR_CHIPS:
            greet(ys[dy] + zs[dz] + same)
        return carry

    lax.fori_loop(0, 2, greet_cores, 0)
    greet(slab + 1 - 2 * core)
    for o in range(1, ANGLES):
        pl.semaphore_signal(
            barrier, inc=1, device_id=(lax.rem(angle + o, ANGLES), slab), device_id_type=MESH
        )

    make_toeplitz(toep, toep_near)
    for load in loads:
        load.wait()
    for src, dst in ((col_v, col_d), (colf_v, colf_d), (dist_v, dist_d)):
        deal_columns(src, dst)
    load_weighted(slab, x_v, xs_hi, xs_lo)
    split_parity(xs_hi, xs_lo, z_ref, y_ref)
    deal_rows(slab, start_v, rows_v, frac_v, s_send)

    pl.semaphore_wait(barrier, SLABS - 1 + ANGLES - 1)
    for o in range(1, ANGLES):
        pl.semaphore_signal(
            plane_sem, inc=1, device_id=(lax.rem(angle + o, ANGLES), slab), device_id_type=MESH
        )

    def send(src, dst, send_sem, recv_sem, to_angle, to_slab):
        pltpu.make_async_remote_copy(
            src_ref=src, dst_ref=dst, send_sem=send_sem, recv_sem=recv_sem,
            device_id=(to_angle, to_slab), device_id_type=MESH,
        ).start()

    def send_rows_to(peer):
        send(s_send.at[peer], s_recv.at[slab], s_ssem, s_rsem, angle, peer)

    for dy, dz in FAR_CHIPS:
        for dc in range(2):
            send_rows_to(ys[dy] + zs[dz] + cores[dc])
    send_rows_to(slab + 1 - 2 * core)
    s_recv[slab] = s_send[slab]
    convolve_far(col_d, toep, hot_even, hot_odd, z_ref, y_ref)
    convolve_near(toep_near, z_ref, y_ref)
    round_filtered(y_ref, f_even, f_odd)

    def send_columns(peer):
        send(h_send.at[peer], h_recv.at[slab], h_ssem, h_rsem, angle, peer)

    def tile_at(dy, dz):
        return lax.rem(slab // 8 + dy, 4) * 2 + lax.rem(slab // 4 + dz, 2)

    def columns(turn, carry):
        for i, (dy, dz) in enumerate(
            ((2 + turn, 1), (2 + turn, 0), (1 - turn, 1), (1 - turn, 0))
        ):
            tile = tile_at(dy, dz)
            at = pl.multiple_of(tile * TILE, TILE)
            value = interpolate_columns(
                at, f_even, f_odd, hot_even, hot_odd, col_d, colf_d, dist_d
            ).astype(BF16)
            for j in range(4):
                h_send[tile * 4 + j] = value[:, j * 128 : (j + 1) * 128]
            for j in range(4):
                if i < 3 or j > 0:
                    send_columns(tile * 4 + lax.rem(slab + j, 4))
        return carry

    lax.fori_loop(0, 2, columns, 0)
    send_columns(tile_at(1, 0) * 4 + lax.rem(slab, 4))
    h_recv[slab] = h_send[slab]

    def wait_bytes(ref, count, sem):
        pltpu.make_async_copy(ref.at[pl.ds(0, count)], ref.at[pl.ds(0, count)], sem).wait()

    wait_bytes(s_recv, SLABS - 1, s_rsem)
    transpose_rows(s_recv, st_ref)
    pl.semaphore_wait(plane_sem, ANGLES - 1)
    wait_bytes(h_recv, SLABS - 1, h_rsem)
    tables = make_tables(h_recv)
    slot = angle * 16 + chip
    my_half = slab // 16
    own_y = slab // 8
    other_y = my_half * 4 + 1 - own_y
    for turn in range(2):
        half = 1 - my_half if turn == 0 else my_half
        look_up_half(half, st_ref, tables, o_send)
        rows = (lax.rem(own_y + 2, 4), lax.rem(other_y + 2, 4)) if turn == 0 else (other_y, own_y)
        for i in range(16):
            dz, dc = FAR_LANE[i % 8]
            if turn == 1 and i == 15:
                break
            t = rows[i // 8] * 8 + zs[dz] + cores[dc]
            for e in range(2):
                send(o_send.at[e, t], o_recv.at[slot], o_ssem, o_rsem, core + 2 * e, t)
    for e in range(2):

        @pl.when(core + 2 * e != angle)
        def _():
            send(o_send.at[e, slab], o_recv.at[slot], o_ssem, o_rsem, core + 2 * e, slab)

    @pl.when(at_home)
    def _():
        o_recv[slot] = o_send[angle // 2, slab]
        wait_bytes(o_recv, 63, o_rsem)

    @pl.when(jnp.logical_not(at_home))
    def _():
        wait_bytes(o_recv, 64, o_rsem)

    sum_angles(o_recv, out_ref)

    wait_bytes(s_send, SLABS - 1, s_ssem)
    wait_bytes(h_send, SLABS - 1, h_ssem)

    @pl.when(at_home)
    def _():
        wait_bytes(o_recv, 63, o_ssem)

    @pl.when(jnp.logical_not(at_home))
    def _():
        wait_bytes(o_recv, 64, o_ssem)


SCRATCH = [
    pltpu.VMEM((BANDS, BAND, COLS), F32),
    pltpu.VMEM((1, SLABS), I32),
    pltpu.VMEM((PLANES, VOX), I32),
    pltpu.VMEM((PLANES, VOX), F32),
    pltpu.VMEM((1, VOX), I32),
    pltpu.VMEM((1, VOX), F32),
    pltpu.VMEM((1, VOX), F32),
    pltpu.VMEM((1, VOX), I32),
    pltpu.VMEM((1, VOX), F32),
    pltpu.VMEM((1, VOX), F32),
    pltpu.VMEM((128, TOEP_WIDTH), BF16),
    pltpu.VMEM((2, 128, NEAR_WIDTH), BF16),
    pltpu.VMEM((SUB, VOX), BF16),
    pltpu.VMEM((SUB, VOX), BF16),
    pltpu.VMEM((2 * SUB + ROWS, SUB), BF16),
    pltpu.VMEM((2 * SUB + ROWS, SUB), BF16),
    pltpu.VMEM((2, 2 * SUB, SUB), BF16),
    pltpu.VMEM((2 * SUB, SUB), F32),
    pltpu.VMEM((SUB, SUB), BF16),
    pltpu.VMEM((SUB, SUB), BF16),
    pltpu.VMEM((SLABS, PLANES, 128), F32),
    pltpu.VMEM((SLABS, PLANES, 128), F32),
    pltpu.VMEM((SLABS, ROWS, 128), BF16),
    pltpu.VMEM((SLABS, ROWS, 128), BF16),
    pltpu.VMEM((2, SLABS, 8, 128), F32),
    pltpu.VMEM((2 * SLABS, 8, 128), F32),
    pltpu.VMEM((128, SLABS * PLANES), F32),
    pltpu.SemaphoreType.DMA((7,)),
    pltpu.SemaphoreType.DMA,
    pltpu.SemaphoreType.DMA,
    pltpu.SemaphoreType.DMA,
    pltpu.SemaphoreType.DMA,
    pltpu.SemaphoreType.DMA,
    pltpu.SemaphoreType.DMA,
    pltpu.SemaphoreType.REGULAR,
]


def body(projections, band_start, row_index, row_frac, col_index, col_frac, distance_weight):
    call = pl.pallas_call(
        kernel,
        out_shape=jax.ShapeDtypeStruct((PLANES, OUT_VOX), F32),
        in_specs=[pl.BlockSpec(memory_space=pltpu.HBM)] * 7,
        out_specs=pl.BlockSpec(memory_space=pltpu.VMEM),
        scratch_shapes=SCRATCH,
        compiler_params=pltpu.CompilerParams(
            collective_id=0, has_side_effects=True, vmem_limit_bytes=40 * 1024 * 1024
        ),
        cost_estimate=pl.CostEstimate(
            flops=6 * 10**9, bytes_accessed=2 * 10**6, transcendentals=0
        ),
    )
    operands = (
        projections.reshape(BANDS, BAND, COLS),
        band_start,
        row_index.reshape(PLANES, VOX),
        row_frac.reshape(PLANES, VOX),
        col_index,
        col_frac,
        distance_weight,
    )
    return call(*(pltpu.with_memory_space_constraint(value, pltpu.HBM) for value in operands))


def solution(mesh):
    in_specs = (
        P("angle", None, "slab", None, None),
        P("angle", None),
        P("angle", "slab", None),
        P("angle", "slab", None),
        P("angle", None),
        P("angle", None),
        P("angle", None),
    )
    out_specs = P("slab", "angle")
    return jax.shard_map(body, mesh=mesh, in_specs=in_specs, out_specs=out_specs, check_vma=False)
```

```python
import math

import jax
import jax.numpy as jnp
from jax import lax
from jax.experimental import pallas as pl
from jax.experimental.pallas import tpu as pltpu
from jax.sharding import PartitionSpec as P

F32 = jnp.float32
BF16 = jnp.bfloat16
I32 = jnp.int32
MESH = pl.DeviceIdType.MESH

ANGLES = 4
OWNERS = 4
SLABS = 32
BANDS = 4
BAND = 4
ROWS = 16
COLS = 8192
DET = 512
PLANES = 16
VOX = 4096
OUT_VOX = 1024
SUB = 256
BLOCKS = 16
HALF = COLS // 2
TOEP_LO = -(BLOCKS - 1) * SUB - 128
TOEP_WIDTH = (2 * BLOCKS - 1) * SUB + 128
NEAR = 1
NEAR_LO = -NEAR * SUB - 128
NEAR_WIDTH = (2 * NEAR + 1) * SUB + 128
TILE = 512
FAR_CHIPS = sorted(
    ((dy, dz) for dy in range(4) for dz in range(4) if dy + dz > 0),
    key=lambda at: (-min(at[0], 4 - at[0]) - min(at[1], 4 - at[1]), at),
)
FAR_LANE = [(2, 1), (2, 0), (1, 1), (1, 0), (3, 1), (3, 0), (0, 1), (0, 0)]


def split_hi_lo(value):
    high = value.astype(BF16)
    low = (value - high.astype(F32)).astype(BF16)
    return high, low


def ramp_odd(offset):
    step = (2 * offset - 1).astype(F32)
    return (-1.0 / math.pi**2) / (step * step)


def make_toeplitz(toep, toep_near):
    lane = lax.broadcasted_iota(I32, (128, 128), 1)
    sub = lax.broadcasted_iota(I32, (128, 128), 0)
    base = (2 * (lane - sub + TOEP_LO) - 1).astype(F32)
    skip = (NEAR_LO - TOEP_LO) // 128

    def value(tile):
        step = base + 256.0 * jnp.asarray(tile, I32).astype(F32)
        square = step * step
        guess = pltpu.reciprocal(square, approx=True)
        return guess * (2.0 - square * guess) * (-1.0 / math.pi**2)

    def one(j, carry):
        for i in range(9):
            tile = j * 9 + i
            toep[:, pl.ds(pl.multiple_of(tile * 128, 128), 128)] = value(tile).astype(BF16)
        return carry

    def near(j):
        where = slice(j * 128, (j + 1) * 128)
        high, low = split_hi_lo(value(j + skip))
        toep_near[0, :, where] = high
        toep_near[1, :, where] = low

    lax.fori_loop(0, TOEP_WIDTH // 1152, one, 0)
    for j in range(NEAR_WIDTH // 128):
        near(j)


def make_hot(n, col_d, hot_even, hot_odd):
    lanes = slice(n * SUB, (n + 1) * SUB)
    column = col_d[:, lanes]
    row = lax.broadcasted_iota(I32, (SUB, SUB), 0).astype(F32).astype(BF16)
    one = jnp.ones((SUB, SUB), BF16)
    zero = jnp.zeros((SUB, SUB), BF16)
    for hot, index in (
        (hot_even, lax.shift_right_logical(column + 1, 1)),
        (hot_odd, lax.shift_right_logical(column, 1)),
    ):
        low = jnp.bitwise_and(index, SUB - 1).astype(F32).astype(BF16)
        hot[:, lanes] = jnp.where(row == low, one, zero)


def load_weighted(slab, x_ref, xs_hi, xs_lo):
    scale = 2.0 * COLS
    row = lax.broadcasted_iota(I32, (ROWS, SUB), 0)
    lane = lax.broadcasted_iota(I32, (ROWS, SUB), 1)
    det = ((row // BAND) * SLABS + slab) * BAND + row % BAND
    down = det.astype(F32) - (DET - 1) / 2.0
    rest = scale * scale + down * down
    for kb in range(COLS // SUB):
        across = (lane + kb * SUB).astype(F32) - (COLS - 1) / 2.0
        raw = jnp.concatenate(
            [x_ref[b, :, kb * SUB : (kb + 1) * SUB] for b in range(BANDS)], axis=0
        )
        high, low = split_hi_lo(raw * (scale / jnp.sqrt(rest + across * across)))
        xs_hi[kb * ROWS : (kb + 1) * ROWS, :] = high
        xs_lo[kb * ROWS : (kb + 1) * ROWS, :] = low
    xs_hi[2 * SUB :, :] = jnp.zeros((ROWS, SUB), BF16)
    xs_lo[2 * SUB :, :] = jnp.zeros((ROWS, SUB), BF16)


def one_hot(mask):
    return jnp.where(mask, 1.0, 0.0).astype(BF16)


def split_parity(xs_hi, xs_lo, z_ref, y_ref):
    k = lax.broadcasted_iota(I32, (SUB, SUB), 0)
    n = lax.broadcasted_iota(I32, (SUB, SUB), 1)
    even_odd = one_hot(k == jnp.where(n < 128, 2 * n, 2 * n - 255))
    k2 = lax.broadcasted_iota(I32, (2 * SUB, 128), 0)
    n2 = lax.broadcasted_iota(I32, (2 * SUB, 128), 1)
    later = one_hot(k2 == 2 * n2 + 2)
    first = None
    quarter = None
    for part, xs in enumerate((xs_hi, xs_lo)):
        here = xs[: 2 * SUB, :]
        both = jnp.concatenate([here, xs[ROWS : 2 * SUB + ROWS, :]], axis=1)
        eo = jnp.dot(here, even_odd, preferred_element_type=F32)
        es = jnp.dot(both, later, preferred_element_type=F32).astype(BF16)
        eo_b = eo[:, 128:].astype(BF16)
        for kb in range(2 * BLOCKS):
            mb, half = kb // 2, kb % 2
            lanes = slice(half * 128, half * 128 + 128)
            src = slice(kb * ROWS, (kb + 1) * ROWS)
            z_ref[part, mb * 32 : mb * 32 + 16, lanes] = eo_b[src]
            z_ref[part, mb * 32 + 16 : mb * 32 + 32, lanes] = es[src]
        quarter = eo if quarter is None else quarter + eo
        first = eo[:ROWS, 0:1] if first is None else first + eo[:ROWS, 0:1]
    quarter = quarter * 0.25
    lane = lax.broadcasted_iota(I32, (ROWS, 128), 1)
    for kb in range(2 * BLOCKS):
        mb, half = kb // 2, kb % 2
        lanes = slice(half * 128, half * 128 + 128)
        src = slice(kb * ROWS, (kb + 1) * ROWS)
        y_ref[mb * 32 : mb * 32 + 16, lanes] = quarter[src, :128]
        edge = first * ramp_odd(lane + (kb * 128 + 1))
        y_ref[mb * 32 + 16 : mb * 32 + 32, lanes] = quarter[src, 128:] + edge


def add_block(d, count, table, z_part, y_ref):
    src = max(0, -d) * 32
    dst = max(0, d) * 32
    y_ref[dst : dst + count, :] += jnp.dot(
        z_part[src : src + count, :], table, preferred_element_type=F32
    )


def two_rows(toep, at):
    return jnp.concatenate([toep[:, at : at + SUB], toep[:, at - 128 : at + 128]], axis=0)


def convolve_far(col_d, toep, hot_even, hot_odd, z_ref, y_ref):
    step = 0
    for d in range(-(BLOCKS - 1), BLOCKS):
        if abs(d) > NEAR:
            table = two_rows(toep, d * SUB - TOEP_LO)
            add_block(d, (BLOCKS - abs(d)) * 32, table, z_ref.at[0], y_ref)
            if step < VOX // SUB:
                make_hot(step, col_d, hot_even, hot_odd)
            step += 1


def convolve_near(toep_near, z_ref, y_ref):
    for d in range(-NEAR, NEAR + 1):
        for z_at, t_at in ((0, 0), (1, 0), (0, 1)):
            table = two_rows(toep_near.at[t_at], d * SUB - NEAR_LO)
            add_block(d, (BLOCKS - abs(d)) * 32, table, z_ref.at[z_at], y_ref)


def round_filtered(y_ref, f_even, f_odd):
    for mb in range(BLOCKS):
        f_even[mb * 16 : mb * 16 + 16, :] = y_ref[mb * 32 : mb * 32 + 16, :].astype(BF16)
        f_odd[mb * 16 : mb * 16 + 16, :] = y_ref[mb * 32 + 16 : mb * 32 + 32, :].astype(BF16)


def pick_columns(f_ref, hot, index):
    high16 = jnp.broadcast_to(lax.shift_right_logical(index, 8), (ROWS, TILE))
    wide = jnp.dot(f_ref[...], hot, preferred_element_type=F32)
    got = wide[:ROWS]
    for mb in range(1, BLOCKS):
        got = jnp.where(high16 == mb, wide[mb * ROWS : (mb + 1) * ROWS], got)
    return got


def interpolate_columns(at, f_even, f_odd, hot_even, hot_odd, c_ref, b_ref, w_ref):
    where = pl.ds(at, TILE)
    column = c_ref[:, where]
    frac = b_ref[:, where]
    weight = w_ref[:, where]
    odd = jnp.bitwise_and(column, 1) == 1
    even_weight = jnp.where(odd, frac, 1.0 - frac) * weight
    odd_weight = jnp.where(odd, 1.0 - frac, frac) * weight
    even_part = pick_columns(f_even, hot_even[:, where], lax.shift_right_logical(column + 1, 1))
    odd_part = pick_columns(f_odd, hot_odd[:, where], lax.shift_right_logical(column, 1))
    return even_part * even_weight + odd_part * odd_weight


def pair_halves(read, k, core):
    first = core * OUT_VOX + k * 64
    second = first + 2 * OUT_VOX
    return jnp.concatenate([read(first), read(second)], axis=1)


def deal_columns(src, dst):
    for s in range(SLABS):
        dst[:, s * 128 : (s + 1) * 128] = pair_halves(
            lambda at: src[:, at : at + 64], s // 2, s % 2
        )


def deal_rows(slab, start_v, rows_v, frac_v, s_send):
    lane = lax.broadcasted_iota(I32, (1, SLABS), 1)
    first_row = BAND * jnp.sum(jnp.where(lane == slab, start_v[...], 0), axis=1, keepdims=True)
    for q in range(OWNERS):
        lanes = slice(q * OUT_VOX, (q + 1) * OUT_VOX)
        position = (rows_v[:, lanes] + first_row).astype(F32) + frac_v[:, lanes]
        for k in range(16):
            half = slice((q // 2) * 64, (q // 2) * 64 + 64)
            s_send[2 * k + q % 2, :, half] = position[:, k * 64 : k * 64 + 64]


def transpose_rows(s_recv, st_ref, low_ref, high_ref):
    def one(i, carry):
        zh, th = i // 2, i % 2
        block = s_recv[pl.ds(th * 16, 16), pl.ds(pl.multiple_of(zh * 8, 8), 8), :]
        position = block.reshape(128, 128).T
        row = position.astype(I32)
        lanes = pl.ds(pl.multiple_of(i * 128, 128), 128)
        st_ref[:, lanes] = position - row.astype(F32)
        for ref, r in ((low_ref, row), (high_ref, jnp.minimum(row + 1, DET - 1))):
            ref[:, lanes] = (
                jnp.bitwise_and(lax.shift_right_logical(r, 2), 31) * 16
                + lax.shift_right_logical(r, 7) * 4
                + jnp.bitwise_and(r, 3)
            )
        return carry

    lax.fori_loop(0, 4, one, 0)


def make_tables(h_recv):
    return [h_recv[g * 8 : (g + 1) * 8].reshape(128, 128).astype(F32).T for g in range(4)]


def look_up(frac, places, tables, v):
    values = []
    for place in places:
        lane = jnp.bitwise_and(place, 127)
        which = lax.shift_right_logical(place, 7)
        got = None
        for k in range(4):
            part = jnp.take_along_axis(
                tables[k][v * 8 : v * 8 + 8], lane, axis=1, mode="promise_in_bounds"
            )
            got = part if got is None else jnp.where(which == k, part, got)
        values.append(got)
    return (1.0 - frac) * values[0] + frac * values[1]


def look_up_half(half, st_ref, low_ref, high_ref, tables, o_send):
    found = []
    for zh in range(2):
        lanes = pl.ds(pl.multiple_of((zh * 2 + half) * 128, 128), 128)
        column = []
        for v in range(16):
            rows = slice(v * 8, v * 8 + 8)
            places = (low_ref[rows, lanes], high_ref[rows, lanes])
            column.append(look_up(st_ref[rows, lanes], places, tables, v))
        found.append(column)
    for e in range(2):
        stack = jnp.concatenate(found[0][e * 8 : e * 8 + 8] + found[1][e * 8 : e * 8 + 8], axis=0)
        o_send[e, pl.ds(half * 16, 16)] = stack.T.reshape(16, 8, 128)


def sum_angles(o_recv, out_ref):
    for m in range(8):
        total = []
        for k in (2 * m, 2 * m + 1):
            total.append(o_recv[k] + o_recv[16 + k] + o_recv[32 + k] + o_recv[48 + k])
        lanes = slice(m * 128, (m + 1) * 128)
        for zh in range(2):
            half = slice(zh * 64, zh * 64 + 64)
            out_ref[zh * 8 : zh * 8 + 8, lanes] = jnp.concatenate(
                [total[0][:, half], total[1][:, half]], axis=1
            )


def kernel(
    x_hbm, start_hbm, rows_hbm, frac_hbm, col_hbm, colf_hbm, dist_hbm, out_ref,
    x_v, start_v, rows_v, frac_v, col_v, colf_v, dist_v,
    col_d, colf_d, dist_d,
    toep, toep_near, hot_even, hot_odd, xs_hi, xs_lo, z_ref, y_ref, f_even, f_odd,
    s_send, s_recv, h_send, h_recv, o_send, o_recv, st_ref, low_ref, high_ref,
    in_sem, s_ssem, s_rsem, h_ssem, h_rsem, o_ssem, o_rsem, plane_sem,
):
    angle = lax.axis_index("angle")
    slab = lax.axis_index("slab")
    chip = slab // 2
    core = slab % 2
    at_home = angle % 2 == core

    ys = [lax.rem(slab // 8 + dy, 4) * 8 for dy in range(4)]
    zs = [lax.rem(chip + dz, 4) * 2 for dz in range(4)]
    cores = (core, 1 - core)

    loads = [
        pltpu.make_async_copy(src, dst, in_sem.at[i])
        for i, (src, dst) in enumerate(
            (
                (x_hbm, x_v),
                (col_hbm, col_v),
                (colf_hbm, colf_v),
                (dist_hbm, dist_v),
                (start_hbm, start_v),
                (rows_hbm, rows_v),
                (frac_hbm, frac_v),
            )
        )
    ]
    barrier = pltpu.get_barrier_semaphore()

    def greet(peer):
        pl.semaphore_signal(barrier, inc=1, device_id=(angle, peer), device_id_type=MESH)

    def greet_cores(turn, carry):
        same = turn * core + (1 - turn) * (1 - core)
        for dy, dz in FAR_CHIPS:
            greet(ys[dy] + zs[dz] + same)
        return carry

    lax.fori_loop(0, 2, greet_cores, 0)
    greet(slab + 1 - 2 * core)
    for o in range(1, ANGLES):
        pl.semaphore_signal(
            barrier, inc=1, device_id=(lax.rem(angle + o, ANGLES), slab), device_id_type=MESH
        )

    for load in loads:
        load.start()

    make_toeplitz(toep, toep_near)
    for load in loads:
        load.wait()
    for src, dst in ((col_v, col_d), (colf_v, colf_d), (dist_v, dist_d)):
        deal_columns(src, dst)
    load_weighted(slab, x_v, xs_hi, xs_lo)
    split_parity(xs_hi, xs_lo, z_ref, y_ref)
    deal_rows(slab, start_v, rows_v, frac_v, s_send)

    pl.semaphore_wait(barrier, SLABS - 1 + ANGLES - 1)
    for o in range(1, ANGLES):
        pl.semaphore_signal(
            plane_sem, inc=1, device_id=(lax.rem(angle + o, ANGLES), slab), device_id_type=MESH
        )

    def send(src, dst, send_sem, recv_sem, to_angle, to_slab):
        pltpu.make_async_remote_copy(
            src_ref=src, dst_ref=dst, send_sem=send_sem, recv_sem=recv_sem,
            device_id=(to_angle, to_slab), device_id_type=MESH,
        ).start()

    def send_rows_to(peer):
        send(s_send.at[peer], s_recv.at[slab], s_ssem, s_rsem, angle, peer)

    @pl.when(slab < SLABS)
    def _():
        for dy, dz in FAR_CHIPS:
            for dc in range(2):
                send_rows_to(ys[dy] + zs[dz] + cores[dc])
        send_rows_to(slab + 1 - 2 * core)
        s_recv[slab] = s_send[slab]

    @pl.when(slab < SLABS)
    def _():
        convolve_far(col_d, toep, hot_even, hot_odd, z_ref, y_ref)

    convolve_near(toep_near, z_ref, y_ref)
    round_filtered(y_ref, f_even, f_odd)

    def send_columns(peer):
        send(h_send.at[peer], h_recv.at[slab], h_ssem, h_rsem, angle, peer)

    def tile_at(dy, dz):
        return lax.rem(slab // 8 + dy, 4) * 2 + lax.rem(slab // 4 + dz, 2)

    def columns(turn, carry):
        for i, (dy, dz) in enumerate(
            ((2 + turn, 1), (2 + turn, 0), (1 - turn, 1), (1 - turn, 0))
        ):
            tile = tile_at(dy, dz)
            at = pl.multiple_of(tile * TILE, TILE)
            value = interpolate_columns(
                at, f_even, f_odd, hot_even, hot_odd, col_d, colf_d, dist_d
            ).astype(BF16)
            for j in range(4):
                h_send[tile * 4 + j] = value[:, j * 128 : (j + 1) * 128]
            for j in range(4):
                if i < 3 or j > 0:
                    send_columns(tile * 4 + lax.rem(slab + j, 4))
        return carry

    lax.fori_loop(0, 2, columns, 0)
    send_columns(tile_at(1, 0) * 4 + lax.rem(slab, 4))
    h_recv[slab] = h_send[slab]

    def wait_bytes(ref, count, sem):
        pltpu.make_async_copy(ref.at[pl.ds(0, count)], ref.at[pl.ds(0, count)], sem).wait()

    wait_bytes(s_recv, SLABS - 1, s_rsem)
    transpose_rows(s_recv, st_ref, low_ref, high_ref)
    pl.semaphore_wait(plane_sem, ANGLES - 1)
    wait_bytes(h_recv, SLABS - 1, h_rsem)
    tables = make_tables(h_recv)
    slot = angle * 16 + chip
    my_half = slab // 16
    own_y = slab // 8
    other_y = my_half * 4 + 1 - own_y
    for turn in range(2):
        half = 1 - my_half if turn == 0 else my_half
        look_up_half(half, st_ref, low_ref, high_ref, tables, o_send)
        rows = (lax.rem(own_y + 2, 4), lax.rem(other_y + 2, 4)) if turn == 0 else (other_y, own_y)
        for i in range(16):
            dz, dc = FAR_LANE[i % 8]
            if turn == 1 and i == 15:
                break
            t = rows[i // 8] * 8 + zs[dz] + cores[dc]
            for e in range(2):
                send(o_send.at[e, t], o_recv.at[slot], o_ssem, o_rsem, core + 2 * e, t)
    for e in range(2):

        @pl.when(core + 2 * e != angle)
        def _():
            send(o_send.at[e, slab], o_recv.at[slot], o_ssem, o_rsem, core + 2 * e, slab)

    @pl.when(at_home)
    def _():
        o_recv[slot] = o_send[angle // 2, slab]
        wait_bytes(o_recv, 63, o_rsem)

    @pl.when(jnp.logical_not(at_home))
    def _():
        wait_bytes(o_recv, 64, o_rsem)

    sum_angles(o_recv, out_ref)

    wait_bytes(s_send, SLABS - 1, s_ssem)
    wait_bytes(h_send, SLABS - 1, h_ssem)

    @pl.when(at_home)
    def _():
        wait_bytes(o_recv, 63, o_ssem)

    @pl.when(jnp.logical_not(at_home))
    def _():
        wait_bytes(o_recv, 64, o_ssem)


SCRATCH = [
    pltpu.VMEM((BANDS, BAND, COLS), F32),
    pltpu.VMEM((1, SLABS), I32),
    pltpu.VMEM((PLANES, VOX), I32),
    pltpu.VMEM((PLANES, VOX), F32),
    pltpu.VMEM((1, VOX), I32),
    pltpu.VMEM((1, VOX), F32),
    pltpu.VMEM((1, VOX), F32),
    pltpu.VMEM((1, VOX), I32),
    pltpu.VMEM((1, VOX), F32),
    pltpu.VMEM((1, VOX), F32),
    pltpu.VMEM((128, TOEP_WIDTH), BF16),
    pltpu.VMEM((2, 128, NEAR_WIDTH), BF16),
    pltpu.VMEM((SUB, VOX), BF16),
    pltpu.VMEM((SUB, VOX), BF16),
    pltpu.VMEM((2 * SUB + ROWS, SUB), BF16),
    pltpu.VMEM((2 * SUB + ROWS, SUB), BF16),
    pltpu.VMEM((2, 2 * SUB, SUB), BF16),
    pltpu.VMEM((2 * SUB, SUB), F32),
    pltpu.VMEM((SUB, SUB), BF16),
    pltpu.VMEM((SUB, SUB), BF16),
    pltpu.VMEM((SLABS, PLANES, 128), F32),
    pltpu.VMEM((SLABS, PLANES, 128), F32),
    pltpu.VMEM((SLABS, ROWS, 128), BF16),
    pltpu.VMEM((SLABS, ROWS, 128), BF16),
    pltpu.VMEM((2, SLABS, 8, 128), F32),
    pltpu.VMEM((2 * SLABS, 8, 128), F32),
    pltpu.VMEM((128, SLABS * PLANES), F32),
    pltpu.VMEM((128, SLABS * PLANES), I32),
    pltpu.VMEM((128, SLABS * PLANES), I32),
    pltpu.SemaphoreType.DMA((7,)),
    pltpu.SemaphoreType.DMA,
    pltpu.SemaphoreType.DMA,
    pltpu.SemaphoreType.DMA,
    pltpu.SemaphoreType.DMA,
    pltpu.SemaphoreType.DMA,
    pltpu.SemaphoreType.DMA,
    pltpu.SemaphoreType.REGULAR,
]


def body(projections, band_start, row_index, row_frac, col_index, col_frac, distance_weight):
    call = pl.pallas_call(
        kernel,
        out_shape=jax.ShapeDtypeStruct((PLANES, OUT_VOX), F32),
        in_specs=[pl.BlockSpec(memory_space=pltpu.HBM)] * 7,
        out_specs=pl.BlockSpec(memory_space=pltpu.VMEM),
        scratch_shapes=SCRATCH,
        compiler_params=pltpu.CompilerParams(
            collective_id=0, has_side_effects=True, vmem_limit_bytes=40 * 1024 * 1024
        ),
        cost_estimate=pl.CostEstimate(
            flops=6 * 10**9, bytes_accessed=2 * 10**6, transcendentals=0
        ),
    )
    operands = (
        projections.reshape(BANDS, BAND, COLS),
        band_start,
        row_index.reshape(PLANES, VOX),
        row_frac.reshape(PLANES, VOX),
        col_index,
        col_frac,
        distance_weight,
    )
    return call(*(pltpu.with_memory_space_constraint(value, pltpu.HBM) for value in operands))


def solution(mesh):
    in_specs = (
        P("angle", None, "slab", None, None),
        P("angle", None),
        P("angle", "slab", None),
        P("angle", "slab", None),
        P("angle", None),
        P("angle", None),
        P("angle", None),
    )
    out_specs = P("slab", "angle")
    return jax.shard_map(body, mesh=mesh, in_specs=in_specs, out_specs=out_specs, check_vma=False)
```

```python
import math

import jax
import jax.numpy as jnp
from jax import lax
from jax.experimental import pallas as pl
from jax.experimental.pallas import tpu as pltpu
from jax.sharding import PartitionSpec as P

F32 = jnp.float32
BF16 = jnp.bfloat16
I32 = jnp.int32
MESH = pl.DeviceIdType.MESH

ANGLES = 4
OWNERS = 4
SLABS = 32
BANDS = 4
BAND = 4
ROWS = 16
COLS = 8192
DET = 512
PLANES = 16
VOX = 4096
OUT_VOX = 1024
SUB = 256
BLOCKS = 16
HALF = COLS // 2
TOEP_LO = -(BLOCKS - 1) * SUB - 128
TOEP_WIDTH = (2 * BLOCKS - 1) * SUB + 128
NEAR = 1
NEAR_LO = -NEAR * SUB - 128
NEAR_WIDTH = (2 * NEAR + 1) * SUB + 128
TILE = 512
FAR_CHIPS = sorted(
    ((dy, dz) for dy in range(4) for dz in range(4) if dy + dz > 0),
    key=lambda at: (-min(at[0], 4 - at[0]) - min(at[1], 4 - at[1]), at),
)
FAR_LANE = [(2, 1), (2, 0), (1, 1), (1, 0), (3, 1), (3, 0), (0, 1), (0, 0)]


def split_hi_lo(value):
    high = value.astype(BF16)
    low = (value - high.astype(F32)).astype(BF16)
    return high, low


def ramp_odd(offset):
    step = (2 * offset - 1).astype(F32)
    return (-1.0 / math.pi**2) / (step * step)


def make_toeplitz(toep, toep_near):
    lane = lax.broadcasted_iota(I32, (128, 128), 1)
    sub = lax.broadcasted_iota(I32, (128, 128), 0)
    base = (2 * (lane - sub + TOEP_LO) - 1).astype(F32)
    skip = (NEAR_LO - TOEP_LO) // 128

    def value(tile):
        step = base + 256.0 * jnp.asarray(tile, I32).astype(F32)
        square = step * step
        guess = pltpu.reciprocal(square, approx=True)
        return guess * (2.0 - square * guess) * (-1.0 / math.pi**2)

    def one(j, carry):
        for i in range(9):
            tile = j * 9 + i
            toep[:, pl.ds(pl.multiple_of(tile * 128, 128), 128)] = value(tile).astype(BF16)
        return carry

    def near(j):
        where = slice(j * 128, (j + 1) * 128)
        high, low = split_hi_lo(value(j + skip))
        toep_near[0, :, where] = high
        toep_near[1, :, where] = low

    lax.fori_loop(0, TOEP_WIDTH // 1152, one, 0)
    for j in range(NEAR_WIDTH // 128):
        near(j)


def make_hot(n, col_d, hot_even, hot_odd):
    lanes = slice(n * SUB, (n + 1) * SUB)
    column = col_d[:, lanes]
    row = lax.broadcasted_iota(I32, (SUB, SUB), 0).astype(F32).astype(BF16)
    one = jnp.ones((SUB, SUB), BF16)
    zero = jnp.zeros((SUB, SUB), BF16)
    for hot, index in (
        (hot_even, lax.shift_right_logical(column + 1, 1)),
        (hot_odd, lax.shift_right_logical(column, 1)),
    ):
        low = jnp.bitwise_and(index, SUB - 1).astype(F32).astype(BF16)
        hot[:, lanes] = jnp.where(row == low, one, zero)


def load_weighted(slab, x_ref, xs_hi, xs_lo):
    scale = 2.0 * COLS
    row = lax.broadcasted_iota(I32, (ROWS, SUB), 0)
    lane = lax.broadcasted_iota(I32, (ROWS, SUB), 1)
    det = ((row // BAND) * SLABS + slab) * BAND + row % BAND
    down = det.astype(F32) - (DET - 1) / 2.0
    rest = scale * scale + down * down
    for kb in range(COLS // SUB):
        across = (lane + kb * SUB).astype(F32) - (COLS - 1) / 2.0
        raw = jnp.concatenate(
            [x_ref[b, :, kb * SUB : (kb + 1) * SUB] for b in range(BANDS)], axis=0
        )
        high, low = split_hi_lo(raw * (scale / jnp.sqrt(rest + across * across)))
        xs_hi[kb * ROWS : (kb + 1) * ROWS, :] = high
        xs_lo[kb * ROWS : (kb + 1) * ROWS, :] = low
    xs_hi[2 * SUB :, :] = jnp.zeros((ROWS, SUB), BF16)
    xs_lo[2 * SUB :, :] = jnp.zeros((ROWS, SUB), BF16)


def one_hot(mask):
    return jnp.where(mask, 1.0, 0.0).astype(BF16)


def split_parity(xs_hi, xs_lo, z_ref, y_ref):
    k = lax.broadcasted_iota(I32, (SUB, SUB), 0)
    n = lax.broadcasted_iota(I32, (SUB, SUB), 1)
    even_odd = one_hot(k == jnp.where(n < 128, 2 * n, 2 * n - 255))
    k2 = lax.broadcasted_iota(I32, (2 * SUB, 128), 0)
    n2 = lax.broadcasted_iota(I32, (2 * SUB, 128), 1)
    later = one_hot(k2 == 2 * n2 + 2)
    first = None
    quarter = None
    for part, xs in enumerate((xs_hi, xs_lo)):
        here = xs[: 2 * SUB, :]
        both = jnp.concatenate([here, xs[ROWS : 2 * SUB + ROWS, :]], axis=1)
        eo = jnp.dot(here, even_odd, preferred_element_type=F32)
        es = jnp.dot(both, later, preferred_element_type=F32).astype(BF16)
        eo_b = eo[:, 128:].astype(BF16)
        for kb in range(2 * BLOCKS):
            mb, half = kb // 2, kb % 2
            lanes = slice(half * 128, half * 128 + 128)
            src = slice(kb * ROWS, (kb + 1) * ROWS)
            z_ref[part, mb * 32 : mb * 32 + 16, lanes] = eo_b[src]
            z_ref[part, mb * 32 + 16 : mb * 32 + 32, lanes] = es[src]
        quarter = eo if quarter is None else quarter + eo
        first = eo[:ROWS, 0:1] if first is None else first + eo[:ROWS, 0:1]
    quarter = quarter * 0.25
    lane = lax.broadcasted_iota(I32, (ROWS, 128), 1)
    for kb in range(2 * BLOCKS):
        mb, half = kb // 2, kb % 2
        lanes = slice(half * 128, half * 128 + 128)
        src = slice(kb * ROWS, (kb + 1) * ROWS)
        y_ref[mb * 32 : mb * 32 + 16, lanes] = quarter[src, :128]
        edge = first * ramp_odd(lane + (kb * 128 + 1))
        y_ref[mb * 32 + 16 : mb * 32 + 32, lanes] = quarter[src, 128:] + edge


def add_block(d, count, table, z_part, y_ref):
    src = max(0, -d) * 32
    dst = max(0, d) * 32
    y_ref[dst : dst + count, :] += jnp.dot(
        z_part[src : src + count, :], table, preferred_element_type=F32
    )


def two_rows(toep, at):
    return jnp.concatenate([toep[:, at : at + SUB], toep[:, at - 128 : at + 128]], axis=0)


def convolve_far(col_d, toep, hot_even, hot_odd, z_ref, y_ref):
    step = 0
    for d in range(-(BLOCKS - 1), BLOCKS):
        if abs(d) > NEAR:
            table = two_rows(toep, d * SUB - TOEP_LO)
            add_block(d, (BLOCKS - abs(d)) * 32, table, z_ref.at[0], y_ref)
            if BLOCKS - abs(d) > 10:
                make_hot(step, col_d, hot_even, hot_odd)
                step += 1


def convolve_near(col_d, toep_near, hot_even, hot_odd, z_ref, y_ref):
    step = VOX // SUB // 2
    for d in range(-NEAR, NEAR + 1):
        for z_at, t_at in ((0, 0), (1, 0), (0, 1)):
            table = two_rows(toep_near.at[t_at], d * SUB - NEAR_LO)
            add_block(d, (BLOCKS - abs(d)) * 32, table, z_ref.at[z_at], y_ref)
            if step < VOX // SUB:
                make_hot(step, col_d, hot_even, hot_odd)
            step += 1


def round_filtered(y_ref, f_even, f_odd):
    for mb in range(BLOCKS):
        f_even[mb * 16 : mb * 16 + 16, :] = y_ref[mb * 32 : mb * 32 + 16, :].astype(BF16)
        f_odd[mb * 16 : mb * 16 + 16, :] = y_ref[mb * 32 + 16 : mb * 32 + 32, :].astype(BF16)


def pick_columns(f_ref, hot, index):
    high16 = jnp.broadcast_to(lax.shift_right_logical(index, 8), (ROWS, TILE))
    wide = jnp.dot(f_ref[...], hot, preferred_element_type=F32)
    got = wide[:ROWS]
    for mb in range(1, BLOCKS):
        got = jnp.where(high16 == mb, wide[mb * ROWS : (mb + 1) * ROWS], got)
    return got


def interpolate_columns(at, f_even, f_odd, hot_even, hot_odd, c_ref, b_ref, w_ref):
    where = pl.ds(at, TILE)
    column = c_ref[:, where]
    frac = b_ref[:, where]
    weight = w_ref[:, where]
    odd = jnp.bitwise_and(column, 1) == 1
    even_weight = jnp.where(odd, frac, 1.0 - frac) * weight
    odd_weight = jnp.where(odd, 1.0 - frac, frac) * weight
    even_part = pick_columns(f_even, hot_even[:, where], lax.shift_right_logical(column + 1, 1))
    odd_part = pick_columns(f_odd, hot_odd[:, where], lax.shift_right_logical(column, 1))
    return even_part * even_weight + odd_part * odd_weight


def pair_halves(read, k, core):
    first = core * OUT_VOX + k * 64
    second = first + 2 * OUT_VOX
    return jnp.concatenate([read(first), read(second)], axis=1)


def deal_columns(src, dst):
    for s in range(SLABS):
        dst[:, s * 128 : (s + 1) * 128] = pair_halves(
            lambda at: src[:, at : at + 64], s // 2, s % 2
        )


def deal_rows(slab, start_v, rows_v, frac_v, s_send):
    lane = lax.broadcasted_iota(I32, (1, SLABS), 1)
    first_row = BAND * jnp.sum(jnp.where(lane == slab, start_v[...], 0), axis=1, keepdims=True)
    for q in range(OWNERS):
        lanes = slice(q * OUT_VOX, (q + 1) * OUT_VOX)
        position = (rows_v[:, lanes] + first_row).astype(F32) + frac_v[:, lanes]
        for k in range(16):
            half = slice((q // 2) * 64, (q // 2) * 64 + 64)
            s_send[2 * k + q % 2, :, half] = position[:, k * 64 : k * 64 + 64]


def transpose_rows(s_recv, st_ref, low_ref, high_ref):
    def one(i, carry):
        zh, th = i // 2, i % 2
        block = s_recv[pl.ds(th * 16, 16), pl.ds(pl.multiple_of(zh * 8, 8), 8), :]
        position = block.reshape(128, 128).T
        row = position.astype(I32)
        lanes = pl.ds(pl.multiple_of(i * 128, 128), 128)
        st_ref[:, lanes] = position - row.astype(F32)
        for ref, r in ((low_ref, row), (high_ref, jnp.minimum(row + 1, DET - 1))):
            ref[:, lanes] = (
                jnp.bitwise_and(lax.shift_right_logical(r, 2), 31) * 16
                + lax.shift_right_logical(r, 7) * 4
                + jnp.bitwise_and(r, 3)
            )
        return carry

    lax.fori_loop(0, 4, one, 0)


def make_tables(h_recv):
    return [h_recv[g * 8 : (g + 1) * 8].reshape(128, 128).astype(F32).T for g in range(4)]


def look_up(frac, places, tables, v):
    values = []
    for place in places:
        lane = jnp.bitwise_and(place, 127)
        which = lax.shift_right_logical(place, 7)
        got = None
        for k in range(4):
            part = jnp.take_along_axis(
                tables[k][v * 8 : v * 8 + 8], lane, axis=1, mode="promise_in_bounds"
            )
            got = part if got is None else jnp.where(which == k, part, got)
        values.append(got)
    return (1.0 - frac) * values[0] + frac * values[1]


def look_up_half(half, st_ref, low_ref, high_ref, tables, o_send):
    found = []
    for zh in range(2):
        lanes = pl.ds(pl.multiple_of((zh * 2 + half) * 128, 128), 128)
        column = []
        for v in range(16):
            rows = slice(v * 8, v * 8 + 8)
            places = (low_ref[rows, lanes], high_ref[rows, lanes])
            column.append(look_up(st_ref[rows, lanes], places, tables, v))
        found.append(column)
    for e in range(2):
        stack = jnp.concatenate(found[0][e * 8 : e * 8 + 8] + found[1][e * 8 : e * 8 + 8], axis=0)
        o_send[e, pl.ds(half * 16, 16)] = stack.T.reshape(16, 8, 128)


def sum_angles(o_recv, out_ref):
    for m in range(8):
        total = []
        for k in (2 * m, 2 * m + 1):
            total.append(o_recv[k] + o_recv[16 + k] + o_recv[32 + k] + o_recv[48 + k])
        lanes = slice(m * 128, (m + 1) * 128)
        for zh in range(2):
            half = slice(zh * 64, zh * 64 + 64)
            out_ref[zh * 8 : zh * 8 + 8, lanes] = jnp.concatenate(
                [total[0][:, half], total[1][:, half]], axis=1
            )


def kernel(
    x_hbm, start_hbm, rows_hbm, frac_hbm, col_hbm, colf_hbm, dist_hbm, out_ref,
    x_v, start_v, rows_v, frac_v, col_v, colf_v, dist_v,
    col_d, colf_d, dist_d,
    toep, toep_near, hot_even, hot_odd, xs_hi, xs_lo, z_ref, y_ref, f_even, f_odd,
    s_send, s_recv, h_send, h_recv, o_send, o_recv, st_ref, low_ref, high_ref,
    in_sem, s_ssem, s_rsem, h_ssem, h_rsem, o_ssem, o_rsem, plane_sem,
):
    angle = lax.axis_index("angle")
    slab = lax.axis_index("slab")
    chip = slab // 2
    core = slab % 2
    at_home = angle % 2 == core

    ys = [lax.rem(slab // 8 + dy, 4) * 8 for dy in range(4)]
    zs = [lax.rem(chip + dz, 4) * 2 for dz in range(4)]
    cores = (core, 1 - core)

    loads = [
        pltpu.make_async_copy(src, dst, in_sem.at[i])
        for i, (src, dst) in enumerate(
            (
                (x_hbm, x_v),
                (col_hbm, col_v),
                (colf_hbm, colf_v),
                (dist_hbm, dist_v),
                (start_hbm, start_v),
                (rows_hbm, rows_v),
                (frac_hbm, frac_v),
            )
        )
    ]
    barrier = pltpu.get_barrier_semaphore()

    def greet(peer):
        pl.semaphore_signal(barrier, inc=1, device_id=(angle, peer), device_id_type=MESH)

    def greet_cores(turn, carry):
        same = turn * core + (1 - turn) * (1 - core)
        for dy, dz in FAR_CHIPS:
            greet(ys[dy] + zs[dz] + same)
        return carry

    lax.fori_loop(0, 2, greet_cores, 0)
    greet(slab + 1 - 2 * core)
    for o in range(1, ANGLES):
        pl.semaphore_signal(
            barrier, inc=1, device_id=(lax.rem(angle + o, ANGLES), slab), device_id_type=MESH
        )

    for load in loads:
        load.start()

    make_toeplitz(toep, toep_near)
    for load in loads:
        load.wait()
    for src, dst in ((col_v, col_d), (colf_v, colf_d), (dist_v, dist_d)):
        deal_columns(src, dst)
    load_weighted(slab, x_v, xs_hi, xs_lo)
    split_parity(xs_hi, xs_lo, z_ref, y_ref)
    deal_rows(slab, start_v, rows_v, frac_v, s_send)

    pl.semaphore_wait(barrier, SLABS - 1 + ANGLES - 1)
    for o in range(1, ANGLES):
        pl.semaphore_signal(
            plane_sem, inc=1, device_id=(lax.rem(angle + o, ANGLES), slab), device_id_type=MESH
        )

    def send(src, dst, send_sem, recv_sem, to_angle, to_slab):
        pltpu.make_async_remote_copy(
            src_ref=src, dst_ref=dst, send_sem=send_sem, recv_sem=recv_sem,
            device_id=(to_angle, to_slab), device_id_type=MESH,
        ).start()

    def send_rows_to(peer):
        send(s_send.at[peer], s_recv.at[slab], s_ssem, s_rsem, angle, peer)

    @pl.when(slab < SLABS)
    def _():
        for dy, dz in FAR_CHIPS:
            for dc in range(2):
                send_rows_to(ys[dy] + zs[dz] + cores[dc])
        send_rows_to(slab + 1 - 2 * core)
        s_recv[slab] = s_send[slab]

    @pl.when(slab < SLABS)
    def _():
        convolve_far(col_d, toep, hot_even, hot_odd, z_ref, y_ref)

    convolve_near(col_d, toep_near, hot_even, hot_odd, z_ref, y_ref)
    round_filtered(y_ref, f_even, f_odd)

    def send_columns(peer):
        send(h_send.at[peer], h_recv.at[slab], h_ssem, h_rsem, angle, peer)

    def tile_at(dy, dz):
        return lax.rem(slab // 8 + dy, 4) * 2 + lax.rem(slab // 4 + dz, 2)

    def columns(turn, carry):
        for i, (dy, dz) in enumerate(
            ((2 + turn, 1), (2 + turn, 0), (1 - turn, 1), (1 - turn, 0))
        ):
            tile = tile_at(dy, dz)
            at = pl.multiple_of(tile * TILE, TILE)
            value = interpolate_columns(
                at, f_even, f_odd, hot_even, hot_odd, col_d, colf_d, dist_d
            ).astype(BF16)
            for j in range(4):
                h_send[tile * 4 + j] = value[:, j * 128 : (j + 1) * 128]
            for j in range(4):
                if i < 3 or j > 0:
                    send_columns(tile * 4 + lax.rem(slab + j, 4))
        return carry

    lax.fori_loop(0, 2, columns, 0)
    send_columns(tile_at(1, 0) * 4 + lax.rem(slab, 4))
    h_recv[slab] = h_send[slab]

    def wait_bytes(ref, count, sem):
        pltpu.make_async_copy(ref.at[pl.ds(0, count)], ref.at[pl.ds(0, count)], sem).wait()

    wait_bytes(s_recv, SLABS - 1, s_rsem)
    transpose_rows(s_recv, st_ref, low_ref, high_ref)
    pl.semaphore_wait(plane_sem, ANGLES - 1)
    wait_bytes(h_recv, SLABS - 1, h_rsem)
    tables = make_tables(h_recv)
    slot = angle * 16 + chip
    my_half = slab // 16
    own_y = slab // 8
    other_y = my_half * 4 + 1 - own_y
    for turn in range(2):
        half = 1 - my_half if turn == 0 else my_half
        look_up_half(half, st_ref, low_ref, high_ref, tables, o_send)
        rows = (lax.rem(own_y + 2, 4), lax.rem(other_y + 2, 4)) if turn == 0 else (other_y, own_y)
        for i in range(16):
            dz, dc = FAR_LANE[i % 8]
            if turn == 1 and i == 15:
                break
            t = rows[i // 8] * 8 + zs[dz] + cores[dc]
            for e in range(2):
                send(o_send.at[e, t], o_recv.at[slot], o_ssem, o_rsem, core + 2 * e, t)
    for e in range(2):

        @pl.when(core + 2 * e != angle)
        def _():
            send(o_send.at[e, slab], o_recv.at[slot], o_ssem, o_rsem, core + 2 * e, slab)

    @pl.when(at_home)
    def _():
        o_recv[slot] = o_send[angle // 2, slab]
        wait_bytes(o_recv, 63, o_rsem)

    @pl.when(jnp.logical_not(at_home))
    def _():
        wait_bytes(o_recv, 64, o_rsem)

    sum_angles(o_recv, out_ref)

    wait_bytes(s_send, SLABS - 1, s_ssem)
    wait_bytes(h_send, SLABS - 1, h_ssem)

    @pl.when(at_home)
    def _():
        wait_bytes(o_recv, 63, o_ssem)

    @pl.when(jnp.logical_not(at_home))
    def _():
        wait_bytes(o_recv, 64, o_ssem)


SCRATCH = [
    pltpu.VMEM((BANDS, BAND, COLS), F32),
    pltpu.VMEM((1, SLABS), I32),
    pltpu.VMEM((PLANES, VOX), I32),
    pltpu.VMEM((PLANES, VOX), F32),
    pltpu.VMEM((1, VOX), I32),
    pltpu.VMEM((1, VOX), F32),
    pltpu.VMEM((1, VOX), F32),
    pltpu.VMEM((1, VOX), I32),
    pltpu.VMEM((1, VOX), F32),
    pltpu.VMEM((1, VOX), F32),
    pltpu.VMEM((128, TOEP_WIDTH), BF16),
    pltpu.VMEM((2, 128, NEAR_WIDTH), BF16),
    pltpu.VMEM((SUB, VOX), BF16),
    pltpu.VMEM((SUB, VOX), BF16),
    pltpu.VMEM((2 * SUB + ROWS, SUB), BF16),
    pltpu.VMEM((2 * SUB + ROWS, SUB), BF16),
    pltpu.VMEM((2, 2 * SUB, SUB), BF16),
    pltpu.VMEM((2 * SUB, SUB), F32),
    pltpu.VMEM((SUB, SUB), BF16),
    pltpu.VMEM((SUB, SUB), BF16),
    pltpu.VMEM((SLABS, PLANES, 128), F32),
    pltpu.VMEM((SLABS, PLANES, 128), F32),
    pltpu.VMEM((SLABS, ROWS, 128), BF16),
    pltpu.VMEM((SLABS, ROWS, 128), BF16),
    pltpu.VMEM((2, SLABS, 8, 128), F32),
    pltpu.VMEM((2 * SLABS, 8, 128), F32),
    pltpu.VMEM((128, SLABS * PLANES), F32),
    pltpu.VMEM((128, SLABS * PLANES), I32),
    pltpu.VMEM((128, SLABS * PLANES), I32),
    pltpu.SemaphoreType.DMA((7,)),
    pltpu.SemaphoreType.DMA,
    pltpu.SemaphoreType.DMA,
    pltpu.SemaphoreType.DMA,
    pltpu.SemaphoreType.DMA,
    pltpu.SemaphoreType.DMA,
    pltpu.SemaphoreType.DMA,
    pltpu.SemaphoreType.REGULAR,
]


def body(projections, band_start, row_index, row_frac, col_index, col_frac, distance_weight):
    call = pl.pallas_call(
        kernel,
        out_shape=jax.ShapeDtypeStruct((PLANES, OUT_VOX), F32),
        in_specs=[pl.BlockSpec(memory_space=pltpu.HBM)] * 7,
        out_specs=pl.BlockSpec(memory_space=pltpu.VMEM),
        scratch_shapes=SCRATCH,
        compiler_params=pltpu.CompilerParams(
            collective_id=0, has_side_effects=True, vmem_limit_bytes=40 * 1024 * 1024
        ),
        cost_estimate=pl.CostEstimate(
            flops=6 * 10**9, bytes_accessed=2 * 10**6, transcendentals=0
        ),
    )
    operands = (
        projections.reshape(BANDS, BAND, COLS),
        band_start,
        row_index.reshape(PLANES, VOX),
        row_frac.reshape(PLANES, VOX),
        col_index,
        col_frac,
        distance_weight,
    )
    return call(*(pltpu.with_memory_space_constraint(value, pltpu.HBM) for value in operands))


def solution(mesh):
    in_specs = (
        P("angle", None, "slab", None, None),
        P("angle", None),
        P("angle", "slab", None),
        P("angle", "slab", None),
        P("angle", None),
        P("angle", None),
        P("angle", None),
    )
    out_specs = P("slab", "angle")
    return jax.shard_map(body, mesh=mesh, in_specs=in_specs, out_specs=out_specs, check_vma=False)
```

```python
import math

import jax
import jax.numpy as jnp
from jax import lax
from jax.experimental import pallas as pl
from jax.experimental.pallas import tpu as pltpu
from jax.sharding import PartitionSpec as P

F32 = jnp.float32
BF16 = jnp.bfloat16
I32 = jnp.int32
MESH = pl.DeviceIdType.MESH

ANGLES = 4
OWNERS = 4
SLABS = 32
BANDS = 4
BAND = 4
ROWS = 16
COLS = 8192
DET = 512
PLANES = 16
VOX = 4096
OUT_VOX = 1024
SUB = 256
BLOCKS = 16
HALF = COLS // 2
TOEP_LO = -(BLOCKS - 1) * SUB - 128
TOEP_WIDTH = (2 * BLOCKS - 1) * SUB + 128
NEAR = 1
NEAR_LO = -NEAR * SUB - 128
NEAR_WIDTH = (2 * NEAR + 1) * SUB + 128
TILE = 512
FAR_CHIPS = sorted(
    ((dy, dz) for dy in range(4) for dz in range(4) if dy + dz > 0),
    key=lambda at: (-min(at[0], 4 - at[0]) - min(at[1], 4 - at[1]), at),
)
FAR_LANE = [(2, 1), (2, 0), (1, 1), (1, 0), (3, 1), (3, 0), (0, 1), (0, 0)]


def split_hi_lo(value):
    high = value.astype(BF16)
    low = (value - high.astype(F32)).astype(BF16)
    return high, low


def ramp_odd(offset):
    step = (2 * offset - 1).astype(F32)
    return (-1.0 / math.pi**2) / (step * step)


def make_toeplitz(toep, toep_near):
    lane = lax.broadcasted_iota(I32, (128, 128), 1)
    sub = lax.broadcasted_iota(I32, (128, 128), 0)
    base = (2 * (lane - sub + TOEP_LO) - 1).astype(F32)
    skip = (NEAR_LO - TOEP_LO) // 128

    def value(tile):
        step = base + 256.0 * jnp.asarray(tile, I32).astype(F32)
        square = step * step
        guess = pltpu.reciprocal(square, approx=True)
        return guess * (2.0 - square * guess) * (-1.0 / math.pi**2)

    def one(j, carry):
        for i in range(9):
            tile = j * 9 + i
            toep[:, pl.ds(pl.multiple_of(tile * 128, 128), 128)] = value(tile).astype(BF16)
        return carry

    def near(j):
        where = slice(j * 128, (j + 1) * 128)
        high, low = split_hi_lo(value(j + skip))
        toep_near[0, :, where] = high
        toep_near[1, :, where] = low

    lax.fori_loop(0, TOEP_WIDTH // 1152, one, 0)
    for j in range(NEAR_WIDTH // 128):
        near(j)


def make_hot(n, col_d, hot_even, hot_odd):
    lanes = slice(n * SUB, (n + 1) * SUB)
    column = col_d[:, lanes]
    row = lax.broadcasted_iota(I32, (SUB, SUB), 0).astype(F32).astype(BF16)
    one = jnp.ones((SUB, SUB), BF16)
    zero = jnp.zeros((SUB, SUB), BF16)
    for hot, index in (
        (hot_even, lax.shift_right_logical(column + 1, 1)),
        (hot_odd, lax.shift_right_logical(column, 1)),
    ):
        low = jnp.bitwise_and(index, SUB - 1).astype(F32).astype(BF16)
        hot[:, lanes] = jnp.where(row == low, one, zero)


def load_weighted(slab, x_ref, xs_hi, xs_lo):
    scale = 2.0 * COLS
    row = lax.broadcasted_iota(I32, (ROWS, SUB), 0)
    lane = lax.broadcasted_iota(I32, (ROWS, SUB), 1)
    det = ((row // BAND) * SLABS + slab) * BAND + row % BAND
    down = det.astype(F32) - (DET - 1) / 2.0
    rest = scale * scale + down * down
    for kb in range(COLS // SUB):
        across = (lane + kb * SUB).astype(F32) - (COLS - 1) / 2.0
        raw = jnp.concatenate(
            [x_ref[b, :, kb * SUB : (kb + 1) * SUB] for b in range(BANDS)], axis=0
        )
        high, low = split_hi_lo(raw * (scale / jnp.sqrt(rest + across * across)))
        xs_hi[kb * ROWS : (kb + 1) * ROWS, :] = high
        xs_lo[kb * ROWS : (kb + 1) * ROWS, :] = low
    xs_hi[2 * SUB :, :] = jnp.zeros((ROWS, SUB), BF16)
    xs_lo[2 * SUB :, :] = jnp.zeros((ROWS, SUB), BF16)


def one_hot(mask):
    return jnp.where(mask, 1.0, 0.0).astype(BF16)


def split_parity(xs_hi, xs_lo, z_ref, y_ref):
    k = lax.broadcasted_iota(I32, (SUB, SUB), 0)
    n = lax.broadcasted_iota(I32, (SUB, SUB), 1)
    even_odd = one_hot(k == jnp.where(n < 128, 2 * n, 2 * n - 255))
    last_lane = lax.broadcasted_iota(I32, (2 * SUB, 128), 1) == 127
    first = None
    quarter = None
    for part, xs in enumerate((xs_hi, xs_lo)):
        here = xs[: 2 * SUB, :]
        eo = jnp.dot(here, even_odd, preferred_element_type=F32)
        turned = pltpu.roll(eo[:, :128], 127, 1)
        following = jnp.concatenate([turned[ROWS:], jnp.zeros((ROWS, 128), F32)], axis=0)
        es = jnp.where(last_lane, following, turned).astype(BF16)
        eo_b = eo[:, 128:].astype(BF16)
        for kb in range(2 * BLOCKS):
            mb, half = kb // 2, kb % 2
            lanes = slice(half * 128, half * 128 + 128)
            src = slice(kb * ROWS, (kb + 1) * ROWS)
            z_ref[part, mb * 32 : mb * 32 + 16, lanes] = eo_b[src]
            z_ref[part, mb * 32 + 16 : mb * 32 + 32, lanes] = es[src]
        quarter = eo if quarter is None else quarter + eo
        first = eo[:ROWS, 0:1] if first is None else first + eo[:ROWS, 0:1]
    quarter = quarter * 0.25
    lane = lax.broadcasted_iota(I32, (ROWS, 128), 1)
    for kb in range(2 * BLOCKS):
        mb, half = kb // 2, kb % 2
        lanes = slice(half * 128, half * 128 + 128)
        src = slice(kb * ROWS, (kb + 1) * ROWS)
        y_ref[mb * 32 : mb * 32 + 16, lanes] = quarter[src, :128]
        edge = first * ramp_odd(lane + (kb * 128 + 1))
        y_ref[mb * 32 + 16 : mb * 32 + 32, lanes] = quarter[src, 128:] + edge


def add_block(d, count, table, z_part, y_ref):
    src = max(0, -d) * 32
    dst = max(0, d) * 32
    y_ref[dst : dst + count, :] += jnp.dot(
        z_part[src : src + count, :], table, preferred_element_type=F32
    )


def two_rows(toep, at):
    return jnp.concatenate([toep[:, at : at + SUB], toep[:, at - 128 : at + 128]], axis=0)


def convolve_far(col_d, toep, hot_even, hot_odd, z_ref, y_ref):
    step = 0
    for d in range(-(BLOCKS - 1), BLOCKS):
        if abs(d) > NEAR:
            table = two_rows(toep, d * SUB - TOEP_LO)
            add_block(d, (BLOCKS - abs(d)) * 32, table, z_ref.at[0], y_ref)
            if step < VOX // SUB:
                make_hot(step, col_d, hot_even, hot_odd)
            step += 1


def convolve_near(toep_near, z_ref, y_ref):
    for d in range(-NEAR, NEAR + 1):
        for z_at, t_at in ((0, 0), (1, 0), (0, 1)):
            table = two_rows(toep_near.at[t_at], d * SUB - NEAR_LO)
            add_block(d, (BLOCKS - abs(d)) * 32, table, z_ref.at[z_at], y_ref)


def round_filtered(y_ref, f_even, f_odd):
    for mb in range(BLOCKS):
        f_even[mb * 16 : mb * 16 + 16, :] = y_ref[mb * 32 : mb * 32 + 16, :].astype(BF16)
        f_odd[mb * 16 : mb * 16 + 16, :] = y_ref[mb * 32 + 16 : mb * 32 + 32, :].astype(BF16)


def pick_columns(f_ref, hot, index):
    high16 = jnp.broadcast_to(lax.shift_right_logical(index, 8), (ROWS, TILE))
    wide = jnp.dot(f_ref[...], hot, preferred_element_type=F32)
    got = wide[:ROWS]
    for mb in range(1, BLOCKS):
        got = jnp.where(high16 == mb, wide[mb * ROWS : (mb + 1) * ROWS], got)
    return got


def interpolate_columns(at, f_even, f_odd, hot_even, hot_odd, c_ref, b_ref, w_ref):
    where = pl.ds(at, TILE)
    column = c_ref[:, where]
    frac = b_ref[:, where]
    weight = w_ref[:, where]
    odd = jnp.bitwise_and(column, 1) == 1
    even_weight = jnp.where(odd, frac, 1.0 - frac) * weight
    odd_weight = jnp.where(odd, 1.0 - frac, frac) * weight
    even_part = pick_columns(f_even, hot_even[:, where], lax.shift_right_logical(column + 1, 1))
    odd_part = pick_columns(f_odd, hot_odd[:, where], lax.shift_right_logical(column, 1))
    return even_part * even_weight + odd_part * odd_weight


def pair_halves(read, k, core):
    first = core * OUT_VOX + k * 64
    second = first + 2 * OUT_VOX
    return jnp.concatenate([read(first), read(second)], axis=1)


def deal_columns(src, dst):
    for s in range(SLABS):
        dst[:, s * 128 : (s + 1) * 128] = pair_halves(
            lambda at: src[:, at : at + 64], s // 2, s % 2
        )


def deal_rows(slab, start_v, rows_v, frac_v, s_send):
    lane = lax.broadcasted_iota(I32, (1, SLABS), 1)
    first_row = BAND * jnp.sum(jnp.where(lane == slab, start_v[...], 0), axis=1, keepdims=True)
    for q in range(OWNERS):
        lanes = slice(q * OUT_VOX, (q + 1) * OUT_VOX)
        position = (rows_v[:, lanes] + first_row).astype(F32) + frac_v[:, lanes]
        for k in range(16):
            half = slice((q // 2) * 64, (q // 2) * 64 + 64)
            s_send[2 * k + q % 2, :, half] = position[:, k * 64 : k * 64 + 64]


def transpose_rows(s_recv, st_ref, low_ref, high_ref):
    def one(i, carry):
        zh, th = i // 2, i % 2
        block = s_recv[pl.ds(th * 16, 16), pl.ds(pl.multiple_of(zh * 8, 8), 8), :]
        position = block.reshape(128, 128).T
        row = position.astype(I32)
        lanes = pl.ds(pl.multiple_of(i * 128, 128), 128)
        st_ref[:, lanes] = position - row.astype(F32)
        for ref, r in ((low_ref, row), (high_ref, jnp.minimum(row + 1, DET - 1))):
            ref[:, lanes] = (
                jnp.bitwise_and(lax.shift_right_logical(r, 2), 31) * 16
                + lax.shift_right_logical(r, 7) * 4
                + jnp.bitwise_and(r, 3)
            )
        return carry

    lax.fori_loop(0, 4, one, 0)


def make_tables(h_recv):
    return [h_recv[g * 8 : (g + 1) * 8].reshape(128, 128).astype(F32).T for g in range(4)]


def look_up(frac, places, tables, v):
    values = []
    for place in places:
        lane = jnp.bitwise_and(place, 127)
        which = lax.shift_right_logical(place, 7)
        got = None
        for k in range(4):
            part = jnp.take_along_axis(
                tables[k][v * 8 : v * 8 + 8], lane, axis=1, mode="promise_in_bounds"
            )
            got = part if got is None else jnp.where(which == k, part, got)
        values.append(got)
    return (1.0 - frac) * values[0] + frac * values[1]


def look_up_half(half, st_ref, low_ref, high_ref, tables, o_send):
    found = []
    for zh in range(2):
        lanes = pl.ds(pl.multiple_of((zh * 2 + half) * 128, 128), 128)
        column = []
        for v in range(16):
            rows = slice(v * 8, v * 8 + 8)
            places = (low_ref[rows, lanes], high_ref[rows, lanes])
            column.append(look_up(st_ref[rows, lanes], places, tables, v))
        found.append(column)
    for e in range(2):
        stack = jnp.concatenate(found[0][e * 8 : e * 8 + 8] + found[1][e * 8 : e * 8 + 8], axis=0)
        o_send[e, pl.ds(half * 16, 16)] = stack.T.reshape(16, 8, 128)


def sum_angles(o_recv, out_ref):
    for m in range(8):
        total = []
        for k in (2 * m, 2 * m + 1):
            total.append(o_recv[k] + o_recv[16 + k] + o_recv[32 + k] + o_recv[48 + k])
        lanes = slice(m * 128, (m + 1) * 128)
        for zh in range(2):
            half = slice(zh * 64, zh * 64 + 64)
            out_ref[zh * 8 : zh * 8 + 8, lanes] = jnp.concatenate(
                [total[0][:, half], total[1][:, half]], axis=1
            )


def kernel(
    x_hbm, start_hbm, rows_hbm, frac_hbm, col_hbm, colf_hbm, dist_hbm, out_ref,
    x_v, start_v, rows_v, frac_v, col_v, colf_v, dist_v,
    col_d, colf_d, dist_d,
    toep, toep_near, hot_even, hot_odd, xs_hi, xs_lo, z_ref, y_ref, f_even, f_odd,
    s_send, s_recv, h_send, h_recv, o_send, o_recv, st_ref, low_ref, high_ref,
    in_sem, s_ssem, s_rsem, h_ssem, h_rsem, o_ssem, o_rsem, plane_sem,
):
    angle = lax.axis_index("angle")
    slab = lax.axis_index("slab")
    chip = slab // 2
    core = slab % 2
    at_home = angle % 2 == core

    ys = [lax.rem(slab // 8 + dy, 4) * 8 for dy in range(4)]
    zs = [lax.rem(chip + dz, 4) * 2 for dz in range(4)]
    cores = (core, 1 - core)

    loads = [
        pltpu.make_async_copy(src, dst, in_sem.at[i])
        for i, (src, dst) in enumerate(
            (
                (x_hbm, x_v),
                (col_hbm, col_v),
                (colf_hbm, colf_v),
                (dist_hbm, dist_v),
                (start_hbm, start_v),
                (rows_hbm, rows_v),
                (frac_hbm, frac_v),
            )
        )
    ]
    barrier = pltpu.get_barrier_semaphore()

    def greet(peer):
        pl.semaphore_signal(barrier, inc=1, device_id=(angle, peer), device_id_type=MESH)

    def greet_cores(turn, carry):
        same = turn * core + (1 - turn) * (1 - core)
        for dy, dz in FAR_CHIPS:
            greet(ys[dy] + zs[dz] + same)
        return carry

    lax.fori_loop(0, 2, greet_cores, 0)
    greet(slab + 1 - 2 * core)
    for o in range(1, ANGLES):
        pl.semaphore_signal(
            barrier, inc=1, device_id=(lax.rem(angle + o, ANGLES), slab), device_id_type=MESH
        )

    for load in loads:
        load.start()

    make_toeplitz(toep, toep_near)
    for load in loads:
        load.wait()
    for src, dst in ((col_v, col_d), (colf_v, colf_d), (dist_v, dist_d)):
        deal_columns(src, dst)
    load_weighted(slab, x_v, xs_hi, xs_lo)
    split_parity(xs_hi, xs_lo, z_ref, y_ref)
    deal_rows(slab, start_v, rows_v, frac_v, s_send)

    pl.semaphore_wait(barrier, SLABS - 1 + ANGLES - 1)
    for o in range(1, ANGLES):
        pl.semaphore_signal(
            plane_sem, inc=1, device_id=(lax.rem(angle + o, ANGLES), slab), device_id_type=MESH
        )

    def send(src, dst, send_sem, recv_sem, to_angle, to_slab):
        pltpu.make_async_remote_copy(
            src_ref=src, dst_ref=dst, send_sem=send_sem, recv_sem=recv_sem,
            device_id=(to_angle, to_slab), device_id_type=MESH,
        ).start()

    def send_rows_to(peer):
        send(s_send.at[peer], s_recv.at[slab], s_ssem, s_rsem, angle, peer)

    @pl.when(slab < SLABS)
    def _():
        for dy, dz in FAR_CHIPS:
            for dc in range(2):
                send_rows_to(ys[dy] + zs[dz] + cores[dc])
        send_rows_to(slab + 1 - 2 * core)
        s_recv[slab] = s_send[slab]

    @pl.when(slab < SLABS)
    def _():
        convolve_far(col_d, toep, hot_even, hot_odd, z_ref, y_ref)

    convolve_near(toep_near, z_ref, y_ref)
    round_filtered(y_ref, f_even, f_odd)

    def send_columns(peer):
        send(h_send.at[peer], h_recv.at[slab], h_ssem, h_rsem, angle, peer)

    def tile_at(dy, dz):
        return lax.rem(slab // 8 + dy, 4) * 2 + lax.rem(slab // 4 + dz, 2)

    def columns(turn, carry):
        for i, (dy, dz) in enumerate(
            ((2 + turn, 1), (2 + turn, 0), (1 - turn, 1), (1 - turn, 0))
        ):
            tile = tile_at(dy, dz)
            at = pl.multiple_of(tile * TILE, TILE)
            value = interpolate_columns(
                at, f_even, f_odd, hot_even, hot_odd, col_d, colf_d, dist_d
            ).astype(BF16)
            for j in range(4):
                h_send[tile * 4 + j] = value[:, j * 128 : (j + 1) * 128]
            for j in range(4):
                if i < 3 or j > 0:
                    send_columns(tile * 4 + lax.rem(slab + j, 4))
        return carry

    lax.fori_loop(0, 2, columns, 0)
    send_columns(tile_at(1, 0) * 4 + lax.rem(slab, 4))
    h_recv[slab] = h_send[slab]

    def wait_bytes(ref, count, sem):
        pltpu.make_async_copy(ref.at[pl.ds(0, count)], ref.at[pl.ds(0, count)], sem).wait()

    wait_bytes(s_recv, SLABS - 1, s_rsem)
    transpose_rows(s_recv, st_ref, low_ref, high_ref)
    pl.semaphore_wait(plane_sem, ANGLES - 1)
    wait_bytes(h_recv, SLABS - 1, h_rsem)
    tables = make_tables(h_recv)
    slot = angle * 16 + chip
    my_half = slab // 16
    own_y = slab // 8
    other_y = my_half * 4 + 1 - own_y
    for turn in range(2):
        half = 1 - my_half if turn == 0 else my_half
        look_up_half(half, st_ref, low_ref, high_ref, tables, o_send)
        rows = (lax.rem(own_y + 2, 4), lax.rem(other_y + 2, 4)) if turn == 0 else (other_y, own_y)
        for i in range(16):
            dz, dc = FAR_LANE[i % 8]
            if turn == 1 and i == 15:
                break
            t = rows[i // 8] * 8 + zs[dz] + cores[dc]
            for e in range(2):
                send(o_send.at[e, t], o_recv.at[slot], o_ssem, o_rsem, core + 2 * e, t)
    for e in range(2):

        @pl.when(core + 2 * e != angle)
        def _():
            send(o_send.at[e, slab], o_recv.at[slot], o_ssem, o_rsem, core + 2 * e, slab)

    @pl.when(at_home)
    def _():
        o_recv[slot] = o_send[angle // 2, slab]
        wait_bytes(o_recv, 63, o_rsem)

    @pl.when(jnp.logical_not(at_home))
    def _():
        wait_bytes(o_recv, 64, o_rsem)

    sum_angles(o_recv, out_ref)

    wait_bytes(s_send, SLABS - 1, s_ssem)
    wait_bytes(h_send, SLABS - 1, h_ssem)

    @pl.when(at_home)
    def _():
        wait_bytes(o_recv, 63, o_ssem)

    @pl.when(jnp.logical_not(at_home))
    def _():
        wait_bytes(o_recv, 64, o_ssem)


SCRATCH = [
    pltpu.VMEM((BANDS, BAND, COLS), F32),
    pltpu.VMEM((1, SLABS), I32),
    pltpu.VMEM((PLANES, VOX), I32),
    pltpu.VMEM((PLANES, VOX), F32),
    pltpu.VMEM((1, VOX), I32),
    pltpu.VMEM((1, VOX), F32),
    pltpu.VMEM((1, VOX), F32),
    pltpu.VMEM((1, VOX), I32),
    pltpu.VMEM((1, VOX), F32),
    pltpu.VMEM((1, VOX), F32),
    pltpu.VMEM((128, TOEP_WIDTH), BF16),
    pltpu.VMEM((2, 128, NEAR_WIDTH), BF16),
    pltpu.VMEM((SUB, VOX), BF16),
    pltpu.VMEM((SUB, VOX), BF16),
    pltpu.VMEM((2 * SUB + ROWS, SUB), BF16),
    pltpu.VMEM((2 * SUB + ROWS, SUB), BF16),
    pltpu.VMEM((2, 2 * SUB, SUB), BF16),
    pltpu.VMEM((2 * SUB, SUB), F32),
    pltpu.VMEM((SUB, SUB), BF16),
    pltpu.VMEM((SUB, SUB), BF16),
    pltpu.VMEM((SLABS, PLANES, 128), F32),
    pltpu.VMEM((SLABS, PLANES, 128), F32),
    pltpu.VMEM((SLABS, ROWS, 128), BF16),
    pltpu.VMEM((SLABS, ROWS, 128), BF16),
    pltpu.VMEM((2, SLABS, 8, 128), F32),
    pltpu.VMEM((2 * SLABS, 8, 128), F32),
    pltpu.VMEM((128, SLABS * PLANES), F32),
    pltpu.VMEM((128, SLABS * PLANES), I32),
    pltpu.VMEM((128, SLABS * PLANES), I32),
    pltpu.SemaphoreType.DMA((7,)),
    pltpu.SemaphoreType.DMA,
    pltpu.SemaphoreType.DMA,
    pltpu.SemaphoreType.DMA,
    pltpu.SemaphoreType.DMA,
    pltpu.SemaphoreType.DMA,
    pltpu.SemaphoreType.DMA,
    pltpu.SemaphoreType.REGULAR,
]


def body(projections, band_start, row_index, row_frac, col_index, col_frac, distance_weight):
    call = pl.pallas_call(
        kernel,
        out_shape=jax.ShapeDtypeStruct((PLANES, OUT_VOX), F32),
        in_specs=[pl.BlockSpec(memory_space=pltpu.HBM)] * 7,
        out_specs=pl.BlockSpec(memory_space=pltpu.VMEM),
        scratch_shapes=SCRATCH,
        compiler_params=pltpu.CompilerParams(
            collective_id=0, has_side_effects=True, vmem_limit_bytes=40 * 1024 * 1024
        ),
        cost_estimate=pl.CostEstimate(
            flops=6 * 10**9, bytes_accessed=2 * 10**6, transcendentals=0
        ),
    )
    operands = (
        projections.reshape(BANDS, BAND, COLS),
        band_start,
        row_index.reshape(PLANES, VOX),
        row_frac.reshape(PLANES, VOX),
        col_index,
        col_frac,
        distance_weight,
    )
    return call(*(pltpu.with_memory_space_constraint(value, pltpu.HBM) for value in operands))


def solution(mesh):
    in_specs = (
        P("angle", None, "slab", None, None),
        P("angle", None),
        P("angle", "slab", None),
        P("angle", "slab", None),
        P("angle", None),
        P("angle", None),
        P("angle", None),
    )
    out_specs = P("slab", "angle")
    return jax.shard_map(body, mesh=mesh, in_specs=in_specs, out_specs=out_specs, check_vma=False)
```
